128 devices in a mesh: kern: 8 (over z, x_lo), strip: 16 (over x_hi, y, core).
Axes of the slice: x: 4 (x_hi: 2, x_lo: 2; x = x_hi * 2 + x_lo), y: 4, z: 4, core: 2. Of those that a mesh axis runs over, the one named last changes fastest.
Arguments:
- mask: bfloat16 [512, 1024], P('strip'), may hold values from 0 to 1
- kernels: bfloat16 [72, 2, 33, 33], P('kern'), may hold values from -0.1875 to 0.1875
- eigen: float32 [72], replicated, may hold values from 0.05 to 1
- focus: int32 [72], replicated, may hold values from 0 to 2, as said below
- target: int32 [512, 1024], P('strip'), may hold values 0 or 1
- pixel_weight: float32 [512, 1024], P('strip'), may hold values from 0.3 to 3
- threshold: float32 [3], replicated, may hold values from 0.15 to 0.27
Outputs:
- gradient: float32 [512, 1024], P('strip', 'kern')
- resist: float32 [3, 512, 1024], P(None, 'strip', 'kern')
The draws below stay inside these ranges and needn't reach their ends.
Inputs may be any that keep to these rules, and one draw needn't show every extreme that they name: Each of the three focus planes is named by exactly 24 systems.
All inputs are finite; a program needn't handle non-finite values. No bound on the sum of `target` on one device may be relied on, other than what follows from the above.
Results may differ from the reference program's by a relative error of at most 0.0019.
Values may be sent and summed in bfloat16 or wider, within the bound.
No kernel may reach another device: no remote copies, remote signals or barrier semaphores. Data moves between devices by JAX's collectives and lax.ppermute only.
A program may use at most 64 MiB of HBM per device.

```python
import math
import jax
import jax.numpy as jnp
from jax import lax

H = 16
KS = 33
SYS = 72
COLS = 1024
NROWS = 512


def draw_focus(key, part):
    key = jax.random.fold_in(key, 7)
    order = jax.random.permutation(key, SYS)
    return (order % 3).astype(jnp.int32)


def touch_ends(array, stream_key, least, high):
    place = [jax.random.randint(jax.random.fold_in(stream_key, axis), (), 0, length) for axis, length in enumerate(array.shape)]
    main_axis = array.shape.index(max(array.shape))
    neighbour = place[:main_axis] + [(place[main_axis] + 1) % array.shape[main_axis]] + place[main_axis + 1:]
    return array.at[tuple(place)].set(least).at[tuple(neighbour)].set(high)


def block_levels(rng, dims, pieces, smallest, top_value):
    loudness, own = 1.0, jax.random.fold_in(rng, 6)
    for position, shards_of in pieces:
        heights = jnp.exp(jax.random.uniform(jax.random.fold_in(own, position), (shards_of,), jnp.float32, smallest / len(pieces), top_value / len(pieces)))
        loudness = loudness * jnp.repeat(heights, dims[position] // shards_of).reshape([-1 if axis == position else 1 for axis in range(len(dims))])
    return loudness


def noise(key, dims, width, bound, cuts=(), kind=jnp.bfloat16):
    values = width * jax.random.normal(key, dims, jnp.float32)
    if cuts:
        values = values * block_levels(key, dims, cuts, -0.22, 0.18)
    return jnp.clip(values, -bound, bound).astype(kind)


def setup_inputs(seed: int = 0) -> dict:
    keys = jax.random.split(jax.random.key(seed), 8)
    mask = jnp.clip(1.0 * jax.random.uniform(keys[0], (NROWS, COLS), jnp.float32) ** block_levels(keys[0], (NROWS, COLS), ((0, 16),), -0.2, 0.2), 0.0, 1.0).astype(jnp.bfloat16)
    kernels = noise(keys[1], (SYS, 2, KS, KS), (KS * KS) ** -0.5, 0.1875, ((0, 8),))
    eigen = jnp.clip(jnp.exp(jax.random.uniform(keys[2], (SYS,), jnp.float32, math.log(0.05), math.log(1.0))), 0.05, 1.0)
    focus = draw_focus(jax.random.fold_in(keys[7], 71), 0)
    target = touch_ends((jax.random.randint(keys[4], (NROWS, COLS), 0, 2) < 1).astype(jnp.int32), jax.random.fold_in(keys[4], 1), 0, 1)
    pixel_weight = jnp.clip(jnp.exp(math.log(3.0) - 2.3025851 * jax.random.uniform(keys[5], (NROWS, COLS), jnp.float32) ** block_levels(keys[5], (NROWS, COLS), ((0, 16),), -0.2, 0.2)), 0.3, 3.0)
    threshold = jnp.clip(jax.random.uniform(keys[6], (3,), jnp.float32, 0.15, 0.27), 0.15, 0.27)
    return {"mask": mask, "kernels": kernels, "eigen": eigen, "focus": focus, "target": target, "pixel_weight": pixel_weight, "threshold": threshold}


STEEP = 20.0


def correlate(source, kernel_taps):
    padding = ((H, H), (H, H))
    result = lax.conv_general_dilated(source[None], kernel_taps, (1, 1), padding, dimension_numbers=("NCHW", "OIHW", "NCHW"), precision=lax.Precision.HIGHEST)
    return result[0]


def reference(mask, kernels, eigen, focus, target, pixel_weight, threshold):
    norm_scale = 3.0 / SYS
    picture = mask.astype(jnp.float32)[None]
    planes = jnp.arange(3, dtype=jnp.int32)

    def fields_of(kernel_pair):
        return correlate(picture, kernel_pair.astype(jnp.float32)[:, None])

    def accumulate(running, record):
        kernel_pair, weight, plane_id = record
        field = fields_of(kernel_pair)
        power = weight * (field[0] * field[0] + field[1] * field[1])
        one_hot = (planes == plane_id).astype(jnp.float32)
        return running + one_hot[:, None, None] * power[None], None

    empty_planes = jnp.zeros((3, NROWS, COLS), jnp.float32)
    summed, _ = lax.scan(accumulate, empty_planes, (kernels, eigen, focus))
    intensity = norm_scale * summed
    resist = jax.nn.sigmoid(STEEP * (intensity - threshold[:, None, None]))
    slopes = pixel_weight[None] * 2.0 * (resist - target.astype(jnp.float32)[None]) * STEEP * resist * (1.0 - resist)

    def adjoin(running, record):
        kernel_pair, weight, plane_id = record
        field = fields_of(kernel_pair)
        one_hot = (planes == plane_id).astype(jnp.float32)
        chosen = jnp.sum(one_hot[:, None, None] * slopes, axis=0)
        factor = 2.0 * weight * norm_scale * chosen
        adjoint = lax.optimization_barrier((factor[None] * field).astype(jnp.bfloat16)).astype(jnp.float32)
        flipped = kernel_pair.astype(jnp.float32)[:, ::-1, ::-1][None]
        return running + correlate(adjoint, flipped)[0], None

    empty_grad = jnp.zeros((NROWS, COLS), jnp.float32)
    gradient, _ = lax.scan(adjoin, empty_grad, (kernels, eigen, focus))
    return gradient, resist
```

```python
import jax
import jax.numpy as jnp
from jax import lax
from jax.experimental import pallas as pl
from jax.experimental.pallas import tpu as pltpu
from jax.sharding import PartitionSpec as P

STEEP = 20.0
F32 = jnp.float32
BF16 = jnp.bfloat16


def iota(shape, dim):
    return lax.broadcasted_iota(jnp.int32, shape, dim)


def step_kernel(
    place_ref, thr_ref, fe_ref, own_ref, up_ref, down_ref, *rest
):
    blocks = rest[:8]
    grad_ref, resist_ref = rest[8:10]
    (rows_ref, lo_ref, hi_ref, main_t, side_t, e_ref, raw_ref, wf_ref, wt_ref, main_a, side_a,
     h_main, h_side, d_ref, tgt_main, tgt_side, res_main, res_side) = rest[10:]
    strip = place_ref[0]
    last = place_ref[1]
    norm_scale = 3.0 / 72

    has_up = (strip > 0).astype(F32)
    has_down = (strip < last).astype(F32)
    rows_ref[96:, :] = jnp.zeros((16, 256), F32)
    rows_ref[:, 128:] = jnp.zeros((112, 128), F32)
    rows_ref[0:32, 0:192] = up_ref[0:32, :] * has_up
    rows_ref[32:64, 0:192] = own_ref[0:32, :]
    rows_ref[64:96, 0:192] = down_ref[0:32, :] * has_down

    for kind in range(2):
        above = up_ref[pl.ds(32 + 16 * kind, 16), 0:160]
        below = down_ref[pl.ds(32 + 16 * kind, 16), 0:160]
        if kind == 1:
            above = above * has_up
            below = below * has_down
        mine = own_ref[pl.ds(32 + 32 * kind, 32), 0:160]
        area = jnp.concatenate([above, mine, below], axis=0)
        tgt_main[kind] = area[:, 0:128]
        tgt_side[kind] = jnp.concatenate(
            [area[8 * g : 8 * g + 8, 128:160] for g in range(8)], axis=1
        )

    lo_ref[...] = jnp.concatenate([rows_ref[8 * g : 8 * g + 56, 128:160] for g in range(8)], axis=1)
    hi_ref[...] = jnp.concatenate([rows_ref[8 * g : 8 * g + 56, 160:192] for g in range(8)], axis=1)

    tap = iota((32, 128), 0)
    lane = iota((32, 128), 1)

    def spread_main(block, _):
        eight = rows_ref[pl.ds(pl.multiple_of(block * 8, 8), 8), :]
        for j in range(8):
            r = block * 8 + j
            left = jnp.broadcast_to(eight[j : j + 1, 0:128], (32, 128))
            right = jnp.broadcast_to(eight[j : j + 1, 128:256], (32, 128))
            left = pltpu.roll(left, 97, 1, stride=1, stride_axis=0)
            right = pltpu.roll(right, 97, 1, stride=1, stride_axis=0)
            both = jnp.where(lane + 31 - tap < 128, left, right).astype(BF16)
            main_t[pl.ds(pl.multiple_of(r * 32 + 1024, 32), 32), 0:128] = both
            main_t[pl.ds(pl.multiple_of(r * 32, 32), 32), 128:256] = both
        return 0

    lax.fori_loop(0, 12, spread_main, 0)

    def spread_side(block, _):
        start = pl.multiple_of(block * 8, 8)
        lows, highs = lo_ref[pl.ds(start, 8), :], hi_ref[pl.ds(start, 8), :]
        for j in range(8):
            for half in range(2):
                cols = slice(128 * half, 128 * half + 128)
                low = jnp.broadcast_to(lows[j : j + 1, cols], (32, 128))
                high = jnp.broadcast_to(highs[j : j + 1, cols], (32, 128))
                low = pltpu.roll(low, 97, 1, stride=1, stride_axis=0)
                high = pltpu.roll(high, 1, 1, stride=1, stride_axis=0)
                both = jnp.where((lane & 31) <= tap, low, high).astype(BF16)
                side_t[pl.ds(pl.multiple_of((block * 8 + j) * 32, 32), 32), cols] = both
        return 0

    lax.fori_loop(0, 5, spread_side, 0)

    for w in range(32):
        e_ref[48 * w : 48 * w + 48, :] = jnp.concatenate(
            [rows_ref[w : w + 48, 32:160], rows_ref[w + 32 : w + 80, 32:160]], axis=1
        ).astype(BF16)
    for w in range(8):
        e_ref[48 * (32 + w) : 48 * (33 + w), :] = hi_ref[w : w + 48, :].astype(BF16)

    fe = fe_ref[...]
    fcol = jnp.transpose(fe)[:, 0:1]
    frow = fe[0:1, :]
    before = (fcol == frow) & (iota((256, 256), 0) < iota((256, 256), 1))
    rank = jnp.sum(jnp.where(before, 1.0, 0.0), axis=0, keepdims=True)
    pos = jnp.where(frow >= 0.0, frow * 48.0 + rank, -1.0)
    pick = jnp.where(iota((256, 256), 0).astype(F32) == pos, 1.0, 0.0)
    eig = jnp.sum(pick * fe[1:2, :], axis=1, keepdims=True)[0:144]
    scale = 2.0 * eig * norm_scale

    raw_ref[...] = jnp.zeros_like(raw_ref)
    for s in range(8):
        raw_ref[32 * s : 32 * s + 18, :] = blocks[s][...]
    taps_f = jnp.dot(pick.astype(BF16), raw_ref[...], preferred_element_type=F32)
    wt_ref[...] = jnp.transpose(taps_f).astype(BF16)
    x = iota((128, 128), 0)
    y = iota((128, 128), 1)
    turn = jnp.where(((x >> 5) == (y >> 5)) & ((x & 31) + (y & 31) == 31), 1.0, 0.0).astype(BF16)
    turn_last = jnp.where(
        ((x < 32) & (x + y == 31)) | ((x >= 32) & (x == y)), 1.0, 0.0
    ).astype(BF16)
    for c in range(9):
        piece = taps_f[0:144, 128 * c : 128 * c + 128].astype(BF16)
        wf_ref[:, 128 * c : 128 * c + 128] = jnp.dot(
            piece, turn_last if c == 8 else turn, preferred_element_type=F32
        ).astype(BF16)

    thr = jnp.concatenate([jnp.full((1, 256), thr_ref[f], F32) for f in range(3)], axis=0)

    def imaged(head, tail, tgt, wgt):
        field = jnp.dot(wf_ref[:, 0:1024], head, preferred_element_type=F32)
        field += jnp.dot(wf_ref[:, 1024:1104], tail, preferred_element_type=F32)
        power = eig * (field * field)
        planes = [
            jnp.sum(power[48 * f : 48 * f + 48], axis=0, keepdims=True) for f in range(3)
        ]
        intensity = norm_scale * jnp.concatenate(planes, axis=0)
        printed = 1.0 / (1.0 + jnp.exp(-STEEP * (intensity - thr)))
        slopes = wgt * 2.0 * (printed - tgt) * STEEP * printed * (1.0 - printed)
        adjoint = jnp.concatenate(
            [
                (scale[48 * f : 48 * f + 48] * slopes[f : f + 1]) * field[48 * f : 48 * f + 48]
                for f in range(3)
            ],
            axis=0,
        ).astype(BF16)
        return printed, adjoint

    def main_window(w, _):
        start = pl.multiple_of(w * 32 + 1024, 32)
        head = main_t[pl.ds(start, 1024), :]
        ones = e_ref[pl.ds(pl.multiple_of(w * 48, 16), 48), :]
        tail = jnp.concatenate([main_t[pl.ds(start + 1024, 32), :], ones], axis=0)
        tgt = jnp.concatenate(
            [tgt_main[0, pl.ds(w, 1), :], tgt_main[0, pl.ds(w + 32, 1), :]], axis=1
        )
        wgt = jnp.concatenate(
            [tgt_main[1, pl.ds(w, 1), :], tgt_main[1, pl.ds(w + 32, 1), :]], axis=1
        )
        printed, adjoint = imaged(head, tail, tgt, wgt)
        main_a[w] = adjoint[:, 0:128]
        main_a[w + 32] = adjoint[:, 128:256]
        for f in range(3):
            res_main[f, pl.ds(w, 1), :] = printed[f : f + 1, 0:128]
            res_main[f, pl.ds(w + 32, 1), :] = printed[f : f + 1, 128:256]
        return 0

    lax.fori_loop(0, 32, main_window, 0, unroll=2)

    for w in range(8):
        head = side_t[32 * w : 32 * w + 1024, :]
        ones = e_ref[1536 + 48 * w : 1584 + 48 * w, :]
        tail = jnp.concatenate([side_t[32 * w + 1024 : 32 * w + 1056, :], ones], axis=0)
        printed, adjoint = imaged(
            head, tail, tgt_side[0, w : w + 1, :], tgt_side[1, w : w + 1, :]
        )
        side_a[w] = adjoint
        for f in range(3):
            res_side[f, w : w + 1, :] = printed[f : f + 1, :]

    for f in range(3):
        edge = jnp.concatenate(
            [res_side[f, :, 32 * g : 32 * g + 16] for g in range(2, 6)], axis=0
        )
        resist_ref[f] = jnp.concatenate([res_main[f, 16:48, 16:128], edge], axis=1)

    h_main[...] = jnp.zeros_like(h_main)
    h_side[...] = jnp.zeros_like(h_side)
    d_ref[...] = jnp.zeros_like(d_ref)
    for p in range(32):
        i = 2 * p
        first, final = max(0, 31 - i), min(32, 63 - i)
        pair = jnp.concatenate([main_a[i], main_a[i + 1]], axis=1)
        spot = 32 * (i + first - 31)
        size = 32 * (final + 1 - first)
        h_main[spot : spot + size, :] += jnp.dot(
            wt_ref[32 * first : 32 * first + size, 0:144], pair, preferred_element_type=F32
        )
        d_ref[i : i + 48, :] += jnp.dot(
            wt_ref[1056:1104, 0:144], pair, preferred_element_type=F32
        )
    for w in range(8):
        h_side[32 * w : 32 * w + 1056, :] += jnp.dot(
            wt_ref[0:1056, 0:144], side_a[w], preferred_element_type=F32
        )

    group = lane >> 5
    for r in range(32):
        body = h_main[32 * r + 32 : 32 * r + 64, 0:128] + h_main[32 * r : 32 * r + 32, 128:256]
        edge = jnp.zeros((32, 128), F32)
        for g in range(8):
            u = r + 32 - 8 * g
            if 0 <= u <= 39:
                cols = slice(128 * (g // 4), 128 * (g // 4) + 128)
                edge += jnp.where(group == g % 4, h_side[32 * u : 32 * u + 32, cols], 0.0)
        edge = edge + pltpu.roll(edge, 64, 1)
        edge = edge + pltpu.roll(edge, 32, 1)
        body = pltpu.roll(body, 96, 1, stride=1, stride_axis=0)
        edge = pltpu.roll(edge, 96, 1, stride=1, stride_axis=0)
        both = jnp.where(lane + 32 - tap < 128, body, edge)
        grad_ref[r : r + 1, :] = (
            jnp.sum(both, axis=0, keepdims=True)
            + d_ref[r + 32 : r + 33, 0:128]
            + d_ref[r + 31 : r + 32, 128:256]
        )


def step_call(place, thr, fe, own, up, down, blocks):
    vmem = pl.BlockSpec(memory_space=pltpu.VMEM)
    smem = pl.BlockSpec(memory_space=pltpu.SMEM)
    return pl.pallas_call(
        step_kernel,
        out_shape=(
            jax.ShapeDtypeStruct((32, 128), F32),
            jax.ShapeDtypeStruct((3, 32, 128), F32),
        ),
        in_specs=[smem, smem] + [vmem] * 12,
        out_specs=(vmem, vmem),
        scratch_shapes=[
            pltpu.VMEM((112, 256), F32),
            pltpu.VMEM((56, 256), F32),
            pltpu.VMEM((56, 256), F32),
            pltpu.VMEM((4096, 256), BF16),
            pltpu.VMEM((1280, 256), BF16),
            pltpu.VMEM((1920, 256), BF16),
            pltpu.VMEM((256, 1152), BF16),
            pltpu.VMEM((144, 1152), BF16),
            pltpu.VMEM((1152, 256), BF16),
            pltpu.VMEM((64, 144, 128), BF16),
            pltpu.VMEM((8, 144, 256), BF16),
            pltpu.VMEM((1056, 256), F32),
            pltpu.VMEM((1280, 256), F32),
            pltpu.VMEM((112, 256), F32),
            pltpu.VMEM((2, 64, 128), F32),
            pltpu.VMEM((2, 8, 256), F32),
            pltpu.VMEM((3, 64, 128), F32),
            pltpu.VMEM((3, 8, 256), F32),
        ],
        compiler_params=pltpu.CompilerParams(vmem_limit_bytes=48 * 1024 * 1024),
    )(place, thr, fe, own, up, down, *blocks)


def flat_taps(kernels):
    count = kernels.shape[0] * 2
    pairs = kernels.reshape(count, 33, 33)
    return jnp.concatenate(
        [
            pairs[:, :, :32].reshape(count, 1056),
            pairs[:, :, 32],
            jnp.zeros((count, 63), BF16),
        ],
        axis=1,
    )


def on_device(mask, kernels, eigen, focus, target, pixel_weight, threshold):
    strips = lax.axis_size("strip")
    strip = lax.axis_index("strip")
    me = lax.axis_index("kern")
    taps = flat_taps(kernels)

    def columns(array, rim):
        wide = jnp.pad(array.astype(F32), ((0, 0), (rim, rim)))
        return lax.dynamic_slice_in_dim(wide, me * 128, 128 + 2 * rim, 1)

    mask_cols = columns(mask, 32)
    target_cols = jnp.pad(columns(target, 16), ((0, 0), (0, 32)))
    weight_cols = jnp.pad(columns(pixel_weight, 16), ((0, 0), (0, 32)))
    own = jnp.concatenate([mask_cols, target_cols, weight_cols], axis=0)
    to_next = jnp.concatenate([mask_cols, target_cols[16:], weight_cols[16:]], axis=0)
    to_prev = jnp.concatenate([mask_cols, target_cols[:16], weight_cols[:16]], axis=0)
    up = lax.ppermute(to_next, "strip", [(i, (i + 1) % strips) for i in range(strips)])
    down = lax.ppermute(to_prev, "strip", [((i + 1) % strips, i) for i in range(strips)])
    blocks = [taps] + [
        lax.ppermute(taps, "kern", [(i, i ^ s) for i in range(8)]) for s in range(1, 8)
    ]

    def reorder(values, fill):
        cube = values.reshape(2, 2, 2, 9)
        for axis, bit in ((0, 4), (1, 2), (2, 1)):
            cube = jnp.where((me & bit) > 0, jnp.flip(cube, axis), cube)
        both = jnp.repeat(cube.reshape(8, 9), 2, axis=1)
        return jnp.pad(both, ((0, 0), (0, 14)), constant_values=fill).reshape(1, 256)

    fe = jnp.concatenate(
        [reorder(focus.astype(F32), -1.0), reorder(eigen, 0.0), jnp.zeros((6, 256), F32)], axis=0
    )
    place = jnp.stack([strip, strip * 0 + strips - 1]).astype(jnp.int32)
    return step_call(place, threshold, fe, own, up, down, blocks)


def solution(mesh):
    placed = (
        P("strip", None),
        P("kern", None, None, None),
        P(),
        P(),
        P("strip", None),
        P("strip", None),
        P(),
    )
    return jax.shard_map(
        on_device,
        mesh=mesh,
        in_specs=placed,
        out_specs=(P("strip", "kern"), P(None, "strip", "kern")),
        check_vma=False,
    )
```

```python
import jax
import jax.numpy as jnp
from jax import lax
from jax.experimental import pallas as pl
from jax.experimental.pallas import tpu as pltpu
from jax.sharding import PartitionSpec as P

STEEP = 20.0
F32 = jnp.float32
BF16 = jnp.bfloat16


def iota(shape, dim):
    return lax.broadcasted_iota(jnp.int32, shape, dim)


def spread_kernel(
    place_ref, fe_ref, own_ref, up_ref, down_ref,
    main_t, side_t, e_ref, tgt_main, tgt_side, pick_ref, eig_ref, rows_ref, lo_ref, hi_ref,
):
    strip = place_ref[0]
    last = place_ref[1]

    has_up = (strip > 0).astype(F32)
    has_down = (strip < last).astype(F32)
    rows_ref[96:, :] = jnp.zeros((16, 256), F32)
    rows_ref[:, 128:] = jnp.zeros((112, 128), F32)
    rows_ref[0:32, 0:192] = up_ref[:, 0:192] * has_up
    rows_ref[32:64, 0:192] = own_ref[0:32, :]
    rows_ref[64:96, 0:192] = down_ref[:, 0:192] * has_down

    for kind in range(2):
        above = up_ref[16 * kind : 16 * kind + 16, 192:352]
        below = down_ref[16 * kind : 16 * kind + 16, 192:352]
        if kind == 1:
            above = above * has_up
            below = below * has_down
        mine = own_ref[32 + 32 * kind : 64 + 32 * kind, 0:160]
        area = jnp.concatenate([above, mine, below], axis=0)
        tgt_main[kind] = area[:, 0:128]
        tgt_side[kind] = jnp.concatenate(
            [area[8 * g : 8 * g + 8, 128:160] for g in range(8)], axis=1
        )

    lo_ref[...] = jnp.concatenate([rows_ref[8 * g : 8 * g + 56, 128:160] for g in range(8)], axis=1)
    hi_ref[...] = jnp.concatenate([rows_ref[8 * g : 8 * g + 56, 160:192] for g in range(8)], axis=1)

    tap = iota((32, 128), 0)
    lane = iota((32, 128), 1)

    def spread_main(block, _, to_left, to_right):
        eight = rows_ref[pl.ds(pl.multiple_of(block * 8, 8), 8), :]
        for j in range(8):
            r = block * 8 + j
            left = jnp.broadcast_to(eight[j : j + 1, 0:128], (32, 128))
            right = jnp.broadcast_to(eight[j : j + 1, 128:256], (32, 128))
            left = pltpu.roll(left, 97, 1, stride=1, stride_axis=0)
            right = pltpu.roll(right, 97, 1, stride=1, stride_axis=0)
            both = jnp.where(lane + 31 - tap < 128, left, right).astype(BF16)
            if to_left:
                main_t[pl.ds(pl.multiple_of(r * 32, 32), 32), 0:128] = both
            if to_right:
                main_t[pl.ds(pl.multiple_of(r * 32 - 1024, 32), 32), 128:256] = both
        return 0

    for span in range(3):
        lax.fori_loop(
            4 * span,
            4 * span + 4,
            lambda block, c: spread_main(block, c, span < 2, span > 0),
            0,
        )

    def spread_side(block, _):
        start = pl.multiple_of(block * 8, 8)
        lows, highs = lo_ref[pl.ds(start, 8), :], hi_ref[pl.ds(start, 8), :]
        for j in range(8):
            for half in range(2):
                cols = slice(128 * half, 128 * half + 128)
                low = jnp.broadcast_to(lows[j : j + 1, cols], (32, 128))
                high = jnp.broadcast_to(highs[j : j + 1, cols], (32, 128))
                low = pltpu.roll(low, 97, 1, stride=1, stride_axis=0)
                high = pltpu.roll(high, 1, 1, stride=1, stride_axis=0)
                both = jnp.where((lane & 31) <= tap, low, high).astype(BF16)
                side_t[pl.ds(pl.multiple_of((block * 8 + j) * 32, 32), 32), cols] = both
        return 0

    lax.fori_loop(0, 5, spread_side, 0)

    for m in range(8):
        e_ref[48 * m : 48 * m + 48, :] = jnp.concatenate(
            [rows_ref[4 * m : 4 * m + 48, 32:160], rows_ref[4 * m + 32 : 4 * m + 80, 32:160]], axis=1
        ).astype(BF16)
    for m in range(2):
        e_ref[48 * (8 + m) : 48 * (9 + m), :] = hi_ref[4 * m : 4 * m + 48, :].astype(BF16)

    fe = fe_ref[...]
    fcol = jnp.transpose(fe)[:, 0:1]
    frow = fe[0:1, :]
    before = (fcol == frow) & (iota((256, 256), 0) < iota((256, 256), 1))
    rank = jnp.sum(jnp.where(before, 1.0, 0.0), axis=0, keepdims=True)
    pos = jnp.where(frow >= 0.0, frow * 48.0 + rank, -1.0)
    pick = jnp.where(iota((256, 256), 0).astype(F32) == pos, 1.0, 0.0)
    pick_ref[...] = pick.astype(BF16)
    eig = jnp.sum(pick * fe[1:2, :], axis=1, keepdims=True)[0:144]
    eig_ref[...] = jnp.broadcast_to(eig, (144, 128))


def step_kernel(
    thr_ref, main_t, side_t, e_ref, tgt_main, tgt_side, pick_ref, eig_ref, four_ref, other_ref,
    grad_ref, resist_ref,
    raw_ref, wf_ref, wt_ref, main_a, side_a, h_main, h_side, d_ref, res_main, res_side,
):
    norm_scale = 3.0 / 72
    tap = iota((32, 128), 0)
    lane = iota((32, 128), 1)
    eig = eig_ref[:, 0:1]

    raw_ref[...] = jnp.zeros_like(raw_ref)
    for s in range(4):
        raw_ref[32 * s : 32 * s + 18, :] = four_ref[s]
        raw_ref[32 * s + 128 : 32 * s + 146, :] = other_ref[s]
    taps_f = jnp.dot(pick_ref[...], raw_ref[...], preferred_element_type=F32)
    wt_ref[...] = jnp.transpose(taps_f).astype(BF16)
    x = iota((128, 128), 0)
    y = iota((128, 128), 1)
    turn = jnp.where(((x >> 5) == (y >> 5)) & ((x & 31) + (y & 31) == 31), 1.0, 0.0).astype(BF16)
    turn_last = jnp.where(
        ((x < 32) & (x + y == 31)) | ((x >= 32) & (x == y)), 1.0, 0.0
    ).astype(BF16)
    turned = [
        jnp.dot(
            taps_f[0:144, 128 * c : 128 * c + 128].astype(BF16),
            turn_last if c == 8 else turn,
            preferred_element_type=F32,
        )
        for c in range(9)
    ]
    lane_w = iota((144, 128), 1)
    final = pltpu.roll(turned[8], 96, 1)
    final = jnp.where(lane_w < 33, final, 0.0)
    turned[8] = jnp.where(lane_w < 32, turned[8], 0.0)
    base = jnp.concatenate(turned, axis=1)
    for w in range(4):
        wf_ref[144 * w : 144 * w + 144, 0:1152] = (
            pltpu.roll(base, 32 * w, 1) if w else base
        ).astype(BF16)
        wf_ref[144 * w : 144 * w + 144, 1152:1280] = (
            pltpu.roll(final, w, 1) if w else final
        ).astype(BF16)

    thr = jnp.concatenate([jnp.full((1, 256), thr_ref[f], F32) for f in range(3)] * 4, axis=0)
    eigs = jnp.concatenate([eig] * 4, axis=0)
    scales = 2.0 * eigs * norm_scale

    def imaged(source, start, ones, tgt, wgt):
        field = jnp.dot(
            wf_ref[:, 0:1024], source[start : start + 1024, :], preferred_element_type=F32
        )
        tail = jnp.concatenate([source[start + 1024 : start + 1152, :], ones], axis=0)
        field += jnp.dot(wf_ref[:, 1024:1200], tail, preferred_element_type=F32)
        power = eigs * (field * field)
        planes = jnp.sum(power.reshape(12, 48, 256), axis=1)
        printed = 1.0 / (1.0 + jnp.exp(-STEEP * (norm_scale * planes - thr)))
        tgt = jnp.concatenate([tgt[v // 3 : v // 3 + 1] for v in range(12)], axis=0)
        wgt = jnp.concatenate([wgt[v // 3 : v // 3 + 1] for v in range(12)], axis=0)
        slopes = wgt * 2.0 * (printed - tgt) * STEEP * printed * (1.0 - printed)
        adjoint = (scales.reshape(12, 48, 1) * slopes[:, None, :]) * field.reshape(12, 48, 256)
        return printed, adjoint.reshape(4, 144, 256).astype(BF16)

    for m in range(8):
        both = [
            jnp.concatenate(
                [tgt_main[kind, 4 * m : 4 * m + 4, :], tgt_main[kind, 4 * m + 32 : 4 * m + 36, :]],
                axis=1,
            )
            for kind in range(2)
        ]
        ones = e_ref[48 * m : 48 * m + 48, :]
        printed, adjoint = imaged(main_t, 128 * m, ones, *both)
        main_a[4 * m : 4 * m + 4] = adjoint[:, :, 0:128]
        main_a[4 * m + 32 : 4 * m + 36] = adjoint[:, :, 128:256]
        for v in range(12):
            w = 4 * m + v // 3
            res_main[v % 3, w : w + 1, :] = printed[v : v + 1, 0:128]
            res_main[v % 3, w + 32 : w + 33, :] = printed[v : v + 1, 128:256]

    for m in range(2):
        both = [tgt_side[kind, 4 * m : 4 * m + 4, :] for kind in range(2)]
        ones = e_ref[48 * (8 + m) : 48 * (9 + m), :]
        printed, adjoint = imaged(side_t, 128 * m, ones, *both)
        side_a[4 * m : 4 * m + 4] = adjoint
        for v in range(12):
            w = 4 * m + v // 3
            res_side[v % 3, w : w + 1, :] = printed[v : v + 1, :]

    for f in range(3):
        edge = jnp.concatenate(
            [res_side[f, :, 32 * g : 32 * g + 16] for g in range(2, 6)], axis=0
        )
        resist_ref[f] = jnp.concatenate([res_main[f, 16:48, 16:128], edge], axis=1)

    h_main[...] = jnp.zeros_like(h_main)
    h_side[...] = jnp.zeros_like(h_side)
    d_ref[...] = jnp.zeros_like(d_ref)
    for p in range(32):
        i = 2 * p
        first, final = max(0, 31 - i), min(32, 63 - i)
        pair = jnp.concatenate([main_a[i], main_a[i + 1]], axis=1)
        spot = 32 * (i + first - 31)
        size = 32 * (final + 1 - first)
        h_main[spot : spot + size, :] += jnp.dot(
            wt_ref[32 * first : 32 * first + size, 0:144], pair, preferred_element_type=F32
        )
        d_ref[i : i + 48, :] += jnp.dot(
            wt_ref[1056:1104, 0:144], pair, preferred_element_type=F32
        )
    for w in range(8):
        h_side[32 * w : 32 * w + 1056, :] += jnp.dot(
            wt_ref[0:1056, 0:144], side_a[w], preferred_element_type=F32
        )

    group = lane >> 5
    for r in range(32):
        body = h_main[32 * r + 32 : 32 * r + 64, 0:128] + h_main[32 * r : 32 * r + 32, 128:256]
        edge = jnp.zeros((32, 128), F32)
        for g in range(8):
            u = r + 32 - 8 * g
            if 0 <= u <= 39:
                cols = slice(128 * (g // 4), 128 * (g // 4) + 128)
                edge += jnp.where(group == g % 4, h_side[32 * u : 32 * u + 32, cols], 0.0)
        edge = edge + pltpu.roll(edge, 64, 1)
        edge = edge + pltpu.roll(edge, 32, 1)
        body = pltpu.roll(body, 96, 1, stride=1, stride_axis=0)
        edge = pltpu.roll(edge, 96, 1, stride=1, stride_axis=0)
        both = jnp.where(lane + 32 - tap < 128, body, edge)
        grad_ref[r : r + 1, :] = (
            jnp.sum(both, axis=0, keepdims=True)
            + d_ref[r + 32 : r + 33, 0:128]
            + d_ref[r + 31 : r + 32, 128:256]
        )


VMEM_SPEC = pl.BlockSpec(memory_space=pltpu.VMEM)
SMEM_SPEC = pl.BlockSpec(memory_space=pltpu.SMEM)
BIG = 40 * 1024 * 1024


def spread_call(place, fe, own, up, down):
    return pl.pallas_call(
        spread_kernel,
        out_shape=(
            jax.ShapeDtypeStruct((2048, 256), BF16),
            jax.ShapeDtypeStruct((1280, 256), BF16),
            jax.ShapeDtypeStruct((480, 256), BF16),
            jax.ShapeDtypeStruct((2, 64, 128), F32),
            jax.ShapeDtypeStruct((2, 8, 256), F32),
            jax.ShapeDtypeStruct((256, 256), BF16),
            jax.ShapeDtypeStruct((144, 128), F32),
        ),
        in_specs=[SMEM_SPEC] + [VMEM_SPEC] * 4,
        out_specs=(VMEM_SPEC,) * 7,
        scratch_shapes=[
            pltpu.VMEM((112, 256), F32),
            pltpu.VMEM((56, 256), F32),
            pltpu.VMEM((56, 256), F32),
        ],
        cost_estimate=pl.CostEstimate(flops=2**31, bytes_accessed=2**21, transcendentals=0),
        compiler_params=pltpu.CompilerParams(vmem_limit_bytes=16 * 1024 * 1024),
    )(place, fe, own, up, down)


def step_call(thr, spread, four, other):
    return pl.pallas_call(
        step_kernel,
        out_shape=(
            jax.ShapeDtypeStruct((32, 128), F32),
            jax.ShapeDtypeStruct((3, 32, 128), F32),
        ),
        in_specs=[SMEM_SPEC] + [VMEM_SPEC] * 9,
        out_specs=(VMEM_SPEC, VMEM_SPEC),
        scratch_shapes=[
            pltpu.VMEM((256, 1152), BF16),
            pltpu.VMEM((576, 1280), BF16),
            pltpu.VMEM((1152, 256), BF16),
            pltpu.VMEM((64, 144, 128), BF16),
            pltpu.VMEM((8, 144, 256), BF16),
            pltpu.VMEM((1056, 256), F32),
            pltpu.VMEM((1280, 256), F32),
            pltpu.VMEM((112, 256), F32),
            pltpu.VMEM((3, 64, 128), F32),
            pltpu.VMEM((3, 8, 256), F32),
        ],
        compiler_params=pltpu.CompilerParams(vmem_limit_bytes=32 * 1024 * 1024),
    )(thr, *spread, four, other)


def flat_taps(kernels):
    count = kernels.shape[0] * 2
    pairs = kernels.reshape(count, 33, 33)
    return jnp.concatenate(
        [
            pairs[:, :, :32].reshape(count, 1056),
            pairs[:, :, 32],
            jnp.zeros((count, 63), BF16),
        ],
        axis=1,
    )


def on_device(mask, kernels, eigen, focus, target, pixel_weight, threshold):
    strips = lax.axis_size("strip")
    strip = lax.axis_index("strip")
    me = lax.axis_index("kern")

    def columns(array, rim):
        wide = jnp.pad(array.astype(F32), ((0, 0), (rim, rim)))
        return lax.dynamic_slice_in_dim(wide, me * 128, 128 + 2 * rim, 1)

    mask_cols = columns(mask, 32)
    target_cols = columns(target, 16)
    weight_cols = columns(pixel_weight, 16)

    def rim_rows(start):
        rows = slice(start, start + 16)
        return jnp.concatenate(
            [mask_cols, jnp.concatenate([target_cols[rows], weight_cols[rows]], axis=0)], axis=1
        )

    up = lax.ppermute(rim_rows(16), "strip", [(i, (i + 1) % strips) for i in range(strips)])
    down = lax.ppermute(rim_rows(0), "strip", [((i + 1) % strips, i) for i in range(strips)])
    own = jnp.concatenate(
        [
            mask_cols,
            jnp.pad(jnp.concatenate([target_cols, weight_cols], axis=0), ((0, 0), (0, 32))),
        ],
        axis=0,
    )

    taps = flat_taps(kernels)
    four = jnp.stack(
        [taps]
        + [lax.ppermute(taps, "kern", [(i, i ^ (2 * s)) for i in range(8)]) for s in range(1, 4)]
    )
    other = lax.ppermute(four, "kern", [(i, i ^ 1) for i in range(8)])

    def reorder(values, fill):
        cube = values.reshape(2, 2, 2, 9)
        for axis, bit in ((0, 4), (1, 2), (2, 1)):
            cube = jnp.where((me & bit) > 0, jnp.flip(cube, axis), cube)
        cube = jnp.moveaxis(cube, 2, 0)
        both = jnp.repeat(cube.reshape(8, 9), 2, axis=1)
        return jnp.pad(both, ((0, 0), (0, 14)), constant_values=fill).reshape(1, 256)

    fe = jnp.concatenate(
        [reorder(focus.astype(F32), -1.0), reorder(eigen, 0.0), jnp.zeros((6, 256), F32)], axis=0
    )
    place = jnp.stack([strip, strip * 0 + strips - 1]).astype(jnp.int32)
    spread = spread_call(place, fe, own, up, down)
    return step_call(threshold, spread, four, other)


def solution(mesh):
    placed = (
        P("strip", None),
        P("kern", None, None, None),
        P(),
        P(),
        P("strip", None),
        P("strip", None),
        P(),
    )
    return jax.shard_map(
        on_device,
        mesh=mesh,
        in_specs=placed,
        out_specs=(P("strip", "kern"), P(None, "strip", "kern")),
        check_vma=False,
    )
```

```python
import jax
import jax.numpy as jnp
from jax import lax
from jax.experimental import pallas as pl
from jax.experimental.pallas import tpu as pltpu
from jax.sharding import PartitionSpec as P

STEEP = 20.0
F32 = jnp.float32
BF16 = jnp.bfloat16


def iota(shape, dim):
    return lax.broadcasted_iota(jnp.int32, shape, dim)


def skewed(eight, j, tap, lane):
    left = jnp.broadcast_to(eight[j : j + 1, 0:128], (32, 128))
    right = jnp.broadcast_to(eight[j : j + 1, 128:256], (32, 128))
    left = pltpu.roll(left, 97, 1, stride=1, stride_axis=0)
    right = pltpu.roll(right, 97, 1, stride=1, stride_axis=0)
    return jnp.where(lane + 31 - tap < 128, left, right).astype(BF16)


def own_kernel(
    thr_ref, focus_ref, eigen_ref, mask_ref,
    center, pick_ref, eig_ref, thrs_ref,
    both_ref, rows_ref, thr_vm, focus_vm, eigen_vm, sems,
):
    me = lax.axis_index("kern")
    copies = [
        pltpu.make_async_copy(src, dst, sems.at[n])
        for n, (src, dst) in enumerate(
            ((thr_ref, thr_vm), (focus_ref, focus_vm), (eigen_ref, eigen_vm))
        )
    ]
    for copy in copies:
        copy.start()
    rows_ref[:, 128:256] = jnp.zeros((32, 128), F32)
    rows_ref[:, 0:192] = mask_ref[...]
    tap = iota((32, 128), 0)
    lane = iota((32, 128), 1)

    def spread_own(block, _):
        eight = rows_ref[pl.ds(pl.multiple_of(block * 8, 8), 8), :]
        for j in range(8):
            spot = pl.multiple_of((block * 8 + j) * 32, 32)
            center[pl.ds(spot, 32), :] = skewed(eight, j, tap, lane)
        return 0

    lax.fori_loop(0, 4, spread_own, 0)

    for copy in copies:
        copy.wait()
    both_ref[...] = jnp.zeros((8, 128), F32)
    both_ref[0:1, 0:72] = focus_vm[...].astype(F32)
    both_ref[1:2, 0:72] = eigen_vm[...]
    listed = jnp.transpose(both_ref[...])
    slot = iota((1, 256), 1)
    block = slot >> 5
    holder = me ^ (2 * (block & 3) + (block >> 2))
    inside = (slot & 31) < 18
    system = jnp.where(inside, 9 * holder + ((slot & 31) >> 1), -1)
    here = iota((128, 256), 0) == system
    frow = jnp.sum(jnp.where(here, listed[:, 0:1], 0.0), axis=0, keepdims=True)
    frow = jnp.where(inside, frow, -1.0)
    erow = jnp.sum(jnp.where(here, listed[:, 1:2], 0.0), axis=0, keepdims=True)
    fcol = jnp.transpose(jnp.broadcast_to(frow, (8, 256)))[:, 0:1]
    before = (fcol == frow) & (iota((256, 256), 0) < iota((256, 256), 1))
    rank = jnp.sum(jnp.where(before, 1.0, 0.0), axis=0, keepdims=True)
    pos = jnp.where(frow >= 0.0, frow * 48.0 + rank, -1.0)
    pick = jnp.where(iota((256, 256), 0).astype(F32) == pos, 1.0, 0.0)
    pick_ref[...] = pick.astype(BF16)
    eig = jnp.sum(pick * erow, axis=1, keepdims=True)[0:144]
    eig_ref[...] = jnp.broadcast_to(eig, (144, 128))
    for v in range(12):
        thrs_ref[v : v + 1, :] = jnp.broadcast_to(thr_vm[0:1, v % 3 : v % 3 + 1], (1, 256))


def spread_kernel(
    center, mask_ref, target_ref, weight_ref, up_ref, down_ref,
    main_t, side_t, e_ref, tgt_main, tgt_side,
    rows_ref, lo_ref, hi_ref,
):
    strip = lax.axis_index("strip")
    last = lax.axis_size("strip") - 1

    has_up = (strip > 0).astype(F32)
    has_down = (strip < last).astype(F32)
    rows_ref[96:, :] = jnp.zeros((16, 256), F32)
    rows_ref[:, 128:] = jnp.zeros((112, 128), F32)
    rows_ref[0:32, 0:192] = up_ref[:, 0:192] * has_up
    rows_ref[32:64, 0:192] = mask_ref[...]
    rows_ref[64:96, 0:192] = down_ref[:, 0:192] * has_down

    for kind in range(2):
        above = up_ref[16 * kind : 16 * kind + 16, 192:352]
        below = down_ref[16 * kind : 16 * kind + 16, 192:352]
        if kind == 1:
            above = above * has_up
            below = below * has_down
        mine = (weight_ref if kind else target_ref)[...]
        area = jnp.concatenate([above, mine, below], axis=0)
        tgt_main[kind] = area[:, 0:128]
        tgt_side[kind] = jnp.concatenate(
            [area[8 * g : 8 * g + 8, 128:160] for g in range(8)], axis=1
        )

    lo_ref[...] = jnp.concatenate([rows_ref[8 * g : 8 * g + 56, 128:160] for g in range(8)], axis=1)
    hi_ref[...] = jnp.concatenate([rows_ref[8 * g : 8 * g + 56, 160:192] for g in range(8)], axis=1)

    tap = iota((32, 128), 0)
    lane = iota((32, 128), 1)

    main_t[1024:2048, 0:128] = center[...]
    main_t[0:1024, 128:256] = center[...]

    def spread_rim(block, _):
        start = pl.multiple_of(block * 8, 8)
        above, below = rows_ref[pl.ds(start, 8), :], rows_ref[pl.ds(start + 64, 8), :]
        for j in range(8):
            spot = pl.multiple_of((block * 8 + j) * 32, 32)
            main_t[pl.ds(spot, 32), 0:128] = skewed(above, j, tap, lane)
            main_t[pl.ds(spot + 1024, 32), 128:256] = skewed(below, j, tap, lane)
        return 0

    lax.fori_loop(0, 4, spread_rim, 0)

    def spread_side(block, _):
        start = pl.multiple_of(block * 8, 8)
        lows, highs = lo_ref[pl.ds(start, 8), :], hi_ref[pl.ds(start, 8), :]
        for j in range(8):
            for half in range(2):
                cols = slice(128 * half, 128 * half + 128)
                low = jnp.broadcast_to(lows[j : j + 1, cols], (32, 128))
                high = jnp.broadcast_to(highs[j : j + 1, cols], (32, 128))
                low = pltpu.roll(low, 97, 1, stride=1, stride_axis=0)
                high = pltpu.roll(high, 1, 1, stride=1, stride_axis=0)
                both = jnp.where((lane & 31) <= tap, low, high).astype(BF16)
                side_t[pl.ds(pl.multiple_of((block * 8 + j) * 32, 32), 32), cols] = both
        return 0

    lax.fori_loop(0, 5, spread_side, 0)

    for m in range(8):
        e_ref[48 * m : 48 * m + 48, :] = jnp.concatenate(
            [rows_ref[4 * m : 4 * m + 48, 32:160], rows_ref[4 * m + 32 : 4 * m + 80, 32:160]], axis=1
        ).astype(BF16)
    for m in range(2):
        e_ref[48 * (8 + m) : 48 * (9 + m), :] = hi_ref[4 * m : 4 * m + 48, :].astype(BF16)


def step_kernel(
    main_t, side_t, e_ref, tgt_main, tgt_side, pick_ref, eig_ref, thrs_ref, four_ref, other_ref,
    grad_ref, resist_ref,
    raw_ref, wf_ref, wt_ref, main_a, side_a, h_main, h_side, d_ref, res_main, res_side,
):
    norm_scale = 3.0 / 72
    tap = iota((32, 128), 0)
    lane = iota((32, 128), 1)
    eig = eig_ref[:, 0:1]

    raw_ref[...] = jnp.zeros_like(raw_ref)
    for s in range(4):
        raw_ref[32 * s : 32 * s + 18, :] = four_ref[s]
        raw_ref[32 * s + 128 : 32 * s + 146, :] = other_ref[s]
    taps_f = jnp.dot(pick_ref[...], raw_ref[...], preferred_element_type=F32)
    wt_ref[...] = jnp.transpose(taps_f).astype(BF16)
    x = iota((128, 128), 0)
    y = iota((128, 128), 1)
    turn = jnp.where(((x >> 5) == (y >> 5)) & ((x & 31) + (y & 31) == 31), 1.0, 0.0).astype(BF16)
    turn_last = jnp.where(
        ((x < 32) & (x + y == 31)) | ((x >= 32) & (x == y)), 1.0, 0.0
    ).astype(BF16)
    turned = [
        jnp.dot(
            taps_f[0:144, 128 * c : 128 * c + 128].astype(BF16),
            turn_last if c == 8 else turn,
            preferred_element_type=F32,
        )
        for c in range(9)
    ]
    lane_w = iota((144, 128), 1)
    final = pltpu.roll(turned[8], 96, 1)
    final = jnp.where(lane_w < 33, final, 0.0)
    turned[8] = jnp.where(lane_w < 32, turned[8], 0.0)
    base = jnp.concatenate(turned, axis=1)
    for w in range(4):
        wf_ref[144 * w : 144 * w + 144, 0:1152] = (
            pltpu.roll(base, 32 * w, 1) if w else base
        ).astype(BF16)
        wf_ref[144 * w : 144 * w + 144, 1152:1280] = (
            pltpu.roll(final, w, 1) if w else final
        ).astype(BF16)

    thr = thrs_ref[...]
    eigs = jnp.concatenate([eig] * 4, axis=0)
    scales = 2.0 * eigs * norm_scale

    def imaged(source, start, ones, tgt, wgt):
        field = jnp.dot(
            wf_ref[:, 0:1024], source[start : start + 1024, :], preferred_element_type=F32
        )
        tail = jnp.concatenate([source[start + 1024 : start + 1152, :], ones], axis=0)
        field += jnp.dot(wf_ref[:, 1024:1200], tail, preferred_element_type=F32)
        power = eigs * (field * field)
        planes = jnp.sum(power.reshape(12, 48, 256), axis=1)
        printed = 1.0 / (1.0 + jnp.exp(-STEEP * (norm_scale * planes - thr)))
        tgt = jnp.concatenate([tgt[v // 3 : v // 3 + 1] for v in range(12)], axis=0)
        wgt = jnp.concatenate([wgt[v // 3 : v // 3 + 1] for v in range(12)], axis=0)
        slopes = wgt * 2.0 * (printed - tgt) * STEEP * printed * (1.0 - printed)
        adjoint = (scales.reshape(12, 48, 1) * slopes[:, None, :]) * field.reshape(12, 48, 256)
        return printed, adjoint.reshape(4, 144, 256).astype(BF16)

    for m in range(8):
        both = [
            jnp.concatenate(
                [tgt_main[kind, 4 * m : 4 * m + 4, :], tgt_main[kind, 4 * m + 32 : 4 * m + 36, :]],
                axis=1,
            )
            for kind in range(2)
        ]
        ones = e_ref[48 * m : 48 * m + 48, :]
        printed, adjoint = imaged(main_t, 128 * m, ones, *both)
        main_a[4 * m : 4 * m + 4] = adjoint[:, :, 0:128]
        main_a[4 * m + 32 : 4 * m + 36] = adjoint[:, :, 128:256]
        for v in range(12):
            w = 4 * m + v // 3
            res_main[v % 3, w : w + 1, :] = printed[v : v + 1, 0:128]
            res_main[v % 3, w + 32 : w + 33, :] = printed[v : v + 1, 128:256]

    for m in range(2):
        both = [tgt_side[kind, 4 * m : 4 * m + 4, :] for kind in range(2)]
        ones = e_ref[48 * (8 + m) : 48 * (9 + m), :]
        printed, adjoint = imaged(side_t, 128 * m, ones, *both)
        side_a[4 * m : 4 * m + 4] = adjoint
        for v in range(12):
            w = 4 * m + v // 3
            res_side[v % 3, w : w + 1, :] = printed[v : v + 1, :]

    for f in range(3):
        edge = jnp.concatenate(
            [res_side[f, :, 32 * g : 32 * g + 16] for g in range(2, 6)], axis=0
        )
        resist_ref[f] = jnp.concatenate([res_main[f, 16:48, 16:128], edge], axis=1)

    h_main[...] = jnp.zeros_like(h_main)
    h_side[...] = jnp.zeros_like(h_side)
    d_ref[...] = jnp.zeros_like(d_ref)
    for p in range(32):
        i = 2 * p
        first, final = max(0, 31 - i), min(32, 63 - i)
        pair = jnp.concatenate([main_a[i], main_a[i + 1]], axis=1)
        spot = 32 * (i + first - 31)
        size = 32 * (final + 1 - first)
        h_main[spot : spot + size, :] += jnp.dot(
            wt_ref[32 * first : 32 * first + size, 0:144], pair, preferred_element_type=F32
        )
        d_ref[i : i + 48, :] += jnp.dot(
            wt_ref[1056:1104, 0:144], pair, preferred_element_type=F32
        )
    for w in range(8):
        h_side[32 * w : 32 * w + 1056, :] += jnp.dot(
            wt_ref[0:1056, 0:144], side_a[w], preferred_element_type=F32
        )

    group = lane >> 5
    for r in range(32):
        body = h_main[32 * r + 32 : 32 * r + 64, 0:128] + h_main[32 * r : 32 * r + 32, 128:256]
        edge = jnp.zeros((32, 128), F32)
        for g in range(8):
            u = r + 32 - 8 * g
            if 0 <= u <= 39:
                cols = slice(128 * (g // 4), 128 * (g // 4) + 128)
                edge += jnp.where(group == g % 4, h_side[32 * u : 32 * u + 32, cols], 0.0)
        edge = edge + pltpu.roll(edge, 64, 1)
        edge = edge + pltpu.roll(edge, 32, 1)
        body = pltpu.roll(body, 96, 1, stride=1, stride_axis=0)
        edge = pltpu.roll(edge, 96, 1, stride=1, stride_axis=0)
        both = jnp.where(lane + 32 - tap < 128, body, edge)
        grad_ref[r : r + 1, :] = (
            jnp.sum(both, axis=0, keepdims=True)
            + d_ref[r + 32 : r + 33, 0:128]
            + d_ref[r + 31 : r + 32, 128:256]
        )


VMEM_SPEC = pl.BlockSpec(memory_space=pltpu.VMEM)


def own_call(*given):
    return pl.pallas_call(
        own_kernel,
        out_shape=(
            jax.ShapeDtypeStruct((1024, 128), BF16),
            jax.ShapeDtypeStruct((256, 256), BF16),
            jax.ShapeDtypeStruct((144, 128), F32),
            jax.ShapeDtypeStruct((12, 256), F32),
        ),
        in_specs=[pl.BlockSpec(memory_space=pl.ANY)] * 3 + [VMEM_SPEC],
        out_specs=(VMEM_SPEC,) * 4,
        scratch_shapes=[
            pltpu.VMEM((8, 128), F32),
            pltpu.VMEM((32, 256), F32),
            pltpu.VMEM((1, 3), F32),
            pltpu.VMEM((1, 72), jnp.int32),
            pltpu.VMEM((1, 72), F32),
            pltpu.SemaphoreType.DMA((3,)),
        ],
        cost_estimate=pl.CostEstimate(flops=2**31, bytes_accessed=2**18, transcendentals=0),
        compiler_params=pltpu.CompilerParams(vmem_limit_bytes=16 * 1024 * 1024),
    )(*given)


def spread_call(*given):
    return pl.pallas_call(
        spread_kernel,
        out_shape=(
            jax.ShapeDtypeStruct((2048, 256), BF16),
            jax.ShapeDtypeStruct((1280, 256), BF16),
            jax.ShapeDtypeStruct((480, 256), BF16),
            jax.ShapeDtypeStruct((2, 64, 128), F32),
            jax.ShapeDtypeStruct((2, 8, 256), F32),
        ),
        in_specs=[VMEM_SPEC] * 6,
        out_specs=(VMEM_SPEC,) * 5,
        scratch_shapes=[
            pltpu.VMEM((112, 256), F32),
            pltpu.VMEM((56, 256), F32),
            pltpu.VMEM((56, 256), F32),
        ],
        cost_estimate=pl.CostEstimate(flops=2**29, bytes_accessed=2**21, transcendentals=0),
        compiler_params=pltpu.CompilerParams(vmem_limit_bytes=16 * 1024 * 1024),
    )(*given)


def step_call(spread, order, four, other):
    return pl.pallas_call(
        step_kernel,
        out_shape=(
            jax.ShapeDtypeStruct((32, 128), F32),
            jax.ShapeDtypeStruct((3, 32, 128), F32),
        ),
        in_specs=[VMEM_SPEC] * 10,
        out_specs=(VMEM_SPEC, VMEM_SPEC),
        scratch_shapes=[
            pltpu.VMEM((256, 1152), BF16),
            pltpu.VMEM((576, 1280), BF16),
            pltpu.VMEM((1152, 256), BF16),
            pltpu.VMEM((64, 144, 128), BF16),
            pltpu.VMEM((8, 144, 256), BF16),
            pltpu.VMEM((1056, 256), F32),
            pltpu.VMEM((1280, 256), F32),
            pltpu.VMEM((112, 256), F32),
            pltpu.VMEM((3, 64, 128), F32),
            pltpu.VMEM((3, 8, 256), F32),
        ],
        compiler_params=pltpu.CompilerParams(vmem_limit_bytes=32 * 1024 * 1024),
    )(*spread, *order, four, other)


def flat_taps(kernels):
    count = kernels.shape[0] * 2
    pairs = kernels.reshape(count, 33, 33)
    return jnp.concatenate(
        [
            pairs[:, :, :32].reshape(count, 1056),
            pairs[:, :, 32],
            jnp.zeros((count, 63), BF16),
        ],
        axis=1,
    )


def on_device(mask, kernels, eigen, focus, target, pixel_weight, threshold):
    strips = lax.axis_size("strip")
    me = lax.axis_index("kern")

    def columns(array, rim, place):
        wide = jnp.pad(array.astype(F32), ((0, 0), (rim, rim)))
        return lax.dynamic_slice_in_dim(wide, place * 128, 128 + 2 * rim, 1)

    def rim_rows(start):
        rows = slice(start, start + 16)
        return jnp.concatenate(
            [
                columns(mask, 32, me),
                jnp.concatenate(
                    [columns(target[rows], 16, me), columns(pixel_weight[rows], 16, me)], axis=0
                ),
            ],
            axis=1,
        )

    ahead = [(i, (i + 1) % strips) for i in range(strips)]
    up = lax.ppermute(rim_rows(16), "strip", ahead)
    down = lax.ppermute(rim_rows(0), "strip", [(b, a) for a, b in ahead])

    taps = flat_taps(kernels)
    four = jnp.stack(
        [taps]
        + [lax.ppermute(taps, "kern", [(i, i ^ (2 * s)) for i in range(8)]) for s in range(1, 4)]
    )
    other = lax.ppermute(four, "kern", [(i, i ^ 1) for i in range(8)])

    own_mask = columns(mask, 32, me)
    center, *order = own_call(
        threshold.reshape(1, 3), focus.reshape(1, 72), eigen.reshape(1, 72), own_mask
    )
    spread = spread_call(
        center, own_mask, columns(target, 16, me), columns(pixel_weight, 16, me), up, down
    )
    return step_call(spread, order, four, other)


def solution(mesh):
    placed = (
        P("strip", None),
        P("kern", None, None, None),
        P(),
        P(),
        P("strip", None),
        P("strip", None),
        P(),
    )
    return jax.shard_map(
        on_device,
        mesh=mesh,
        in_specs=placed,
        out_specs=(P("strip", "kern"), P(None, "strip", "kern")),
        check_vma=False,
    )
```

```python
import jax
import jax.numpy as jnp
from jax import lax
from jax.experimental import pallas as pl
from jax.experimental.pallas import tpu as pltpu
from jax.sharding import PartitionSpec as P

STEEP = 20.0
F32 = jnp.float32
BF16 = jnp.bfloat16


def iota(shape, dim):
    return lax.broadcasted_iota(jnp.int32, shape, dim)


def skewed(eight, j, tap, lane):
    left = jnp.broadcast_to(eight[j : j + 1, 0:128], (32, 128))
    right = jnp.broadcast_to(eight[j : j + 1, 128:256], (32, 128))
    left = pltpu.roll(left, 97, 1, stride=1, stride_axis=0)
    right = pltpu.roll(right, 97, 1, stride=1, stride_axis=0)
    return jnp.where(lane + 31 - tap < 128, left, right).astype(BF16)


def own_kernel(
    thr_ref, focus_ref, eigen_ref, mask_ref,
    center, pick_ref, eig_ref, thrs_ref,
    both_ref, rows_ref, thr_vm, focus_vm, eigen_vm, sems,
):
    me = lax.axis_index("kern")
    copies = [
        pltpu.make_async_copy(src, dst, sems.at[n])
        for n, (src, dst) in enumerate(
            ((thr_ref, thr_vm), (focus_ref, focus_vm), (eigen_ref, eigen_vm))
        )
    ]
    for copy in copies:
        copy.start()
    rows_ref[:, 128:256] = jnp.zeros((32, 128), F32)
    rows_ref[:, 0:192] = mask_ref[...]
    tap = iota((32, 128), 0)
    lane = iota((32, 128), 1)

    def spread_own(block, _):
        eight = rows_ref[pl.ds(pl.multiple_of(block * 8, 8), 8), :]
        for j in range(8):
            spot = pl.multiple_of((block * 8 + j) * 32, 32)
            center[pl.ds(spot, 32), :] = skewed(eight, j, tap, lane)
        return 0

    lax.fori_loop(0, 4, spread_own, 0)

    for copy in copies:
        copy.wait()
    both_ref[...] = jnp.zeros((8, 128), F32)
    both_ref[0:1, 0:72] = focus_vm[...].astype(F32)
    both_ref[1:2, 0:72] = eigen_vm[...]
    listed = jnp.transpose(both_ref[...])
    slot = iota((1, 256), 1)
    block = slot >> 5
    holder = me ^ (2 * (block & 3) + (block >> 2))
    inside = (slot & 31) < 18
    system = jnp.where(inside, 9 * holder + ((slot & 31) >> 1), -1)
    here = iota((128, 256), 0) == system
    frow = jnp.sum(jnp.where(here, listed[:, 0:1], 0.0), axis=0, keepdims=True)
    frow = jnp.where(inside, frow, -1.0)
    erow = jnp.sum(jnp.where(here, listed[:, 1:2], 0.0), axis=0, keepdims=True)
    fcol = jnp.transpose(jnp.broadcast_to(frow, (8, 256)))[:, 0:1]
    before = (fcol == frow) & (iota((256, 256), 0) < iota((256, 256), 1))
    rank = jnp.sum(jnp.where(before, 1.0, 0.0), axis=0, keepdims=True)
    pos = jnp.where(frow >= 0.0, frow * 48.0 + rank, -1.0)
    spot = iota((256, 256), 0)
    spot = jnp.where(spot < 128, spot, 128 + (spot & 15))
    pick = jnp.where(spot.astype(F32) == pos, 1.0, 0.0)
    pick_ref[...] = pick.astype(BF16)
    eig = jnp.sum(pick * erow, axis=1, keepdims=True)[0:144]
    eig_ref[...] = jnp.broadcast_to(eig, (144, 128))
    for v in range(12):
        thrs_ref[v : v + 1, :] = jnp.broadcast_to(thr_vm[0:1, v % 3 : v % 3 + 1], (1, 256))


def spread_kernel(
    center, mask_ref, target_ref, weight_ref, near_ref, far_ref,
    main_t, side_t, e_ref, tgt_main, tgt_side,
    rows_ref, lo_ref, hi_ref, up_ref, down_ref,
):
    strip = lax.axis_index("strip")
    last = lax.axis_size("strip") - 1

    odd = jnp.full((32, 352), strip & 1, jnp.int32) > 0
    up_ref[...] = jnp.where(odd, near_ref[...], far_ref[...])
    down_ref[...] = jnp.where(odd, far_ref[...], near_ref[...])

    has_up = (strip > 0).astype(F32)
    has_down = (strip < last).astype(F32)
    rows_ref[96:, :] = jnp.zeros((16, 256), F32)
    rows_ref[:, 128:] = jnp.zeros((112, 128), F32)
    rows_ref[0:32, 0:192] = up_ref[:, 0:192] * has_up
    rows_ref[32:64, 0:192] = mask_ref[...]
    rows_ref[64:96, 0:192] = down_ref[:, 0:192] * has_down

    for kind in range(2):
        above = up_ref[16 * kind : 16 * kind + 16, 192:352]
        below = down_ref[16 * kind : 16 * kind + 16, 192:352]
        if kind == 1:
            above = above * has_up
            below = below * has_down
        mine = (weight_ref if kind else target_ref)[...]
        area = jnp.concatenate([above, mine, below], axis=0)
        tgt_main[kind] = area[:, 0:128]
        tgt_side[kind] = jnp.concatenate(
            [area[8 * g : 8 * g + 8, 128:160] for g in range(8)], axis=1
        )

    lo_ref[...] = jnp.concatenate([rows_ref[8 * g : 8 * g + 56, 128:160] for g in range(8)], axis=1)
    hi_ref[...] = jnp.concatenate([rows_ref[8 * g : 8 * g + 56, 160:192] for g in range(8)], axis=1)

    tap = iota((32, 128), 0)
    lane = iota((32, 128), 1)

    main_t[1024:2048, 0:128] = center[...]
    main_t[0:1024, 128:256] = center[...]

    def spread_rim(block, _):
        start = pl.multiple_of(block * 8, 8)
        above, below = rows_ref[pl.ds(start, 8), :], rows_ref[pl.ds(start + 64, 8), :]
        for j in range(8):
            spot = pl.multiple_of((block * 8 + j) * 32, 32)
            main_t[pl.ds(spot, 32), 0:128] = skewed(above, j, tap, lane)
            main_t[pl.ds(spot + 1024, 32), 128:256] = skewed(below, j, tap, lane)
        return 0

    lax.fori_loop(0, 4, spread_rim, 0)

    def spread_side(block, _):
        start = pl.multiple_of(block * 8, 8)
        lows, highs = lo_ref[pl.ds(start, 8), :], hi_ref[pl.ds(start, 8), :]
        for j in range(8):
            for half in range(2):
                cols = slice(128 * half, 128 * half + 128)
                low = jnp.broadcast_to(lows[j : j + 1, cols], (32, 128))
                high = jnp.broadcast_to(highs[j : j + 1, cols], (32, 128))
                low = pltpu.roll(low, 97, 1, stride=1, stride_axis=0)
                high = pltpu.roll(high, 1, 1, stride=1, stride_axis=0)
                both = jnp.where((lane & 31) <= tap, low, high).astype(BF16)
                side_t[pl.ds(pl.multiple_of((block * 8 + j) * 32, 32), 32), cols] = both
        return 0

    lax.fori_loop(0, 5, spread_side, 0)

    for m in range(8):
        e_ref[48 * m : 48 * m + 48, :] = jnp.concatenate(
            [rows_ref[4 * m : 4 * m + 48, 32:160], rows_ref[4 * m + 32 : 4 * m + 80, 32:160]], axis=1
        ).astype(BF16)
    for m in range(2):
        e_ref[48 * (8 + m) : 48 * (9 + m), :] = hi_ref[4 * m : 4 * m + 48, :].astype(BF16)


def step_kernel(
    main_t, side_t, e_ref, tgt_main, tgt_side, pick_ref, eig_ref, thrs_ref, four_ref, other_ref,
    grad_ref, resist_ref,
    raw_ref, wf_ref, wt_ref, wc_ref, ws_ref, wcs_ref, main_a, side_a,
    h_main, h_last, h_side, d_ref, d_last, res_main, res_side,
):
    norm_scale = 3.0 / 72
    tap = iota((32, 128), 0)
    lane = iota((32, 128), 1)
    eig = eig_ref[:, 0:1]

    raw_ref[...] = jnp.zeros_like(raw_ref)
    for s in range(4):
        raw_ref[32 * s : 32 * s + 18, :] = four_ref[s]
        raw_ref[32 * s + 128 : 32 * s + 146, :] = other_ref[s]
    taps_f = jnp.dot(pick_ref[...], raw_ref[...], preferred_element_type=F32)
    taps_t = jnp.transpose(taps_f)
    blank = jnp.zeros((32, 128), BF16)
    wt_ref[0:32, :] = blank
    wt_ref[32:1088, :] = taps_t[0:1056, 0:128].astype(BF16)
    wt_ref[1088:1120, :] = blank
    edge_taps = taps_t[1056:1104, 0:128]
    wc_ref[...] = jnp.concatenate([edge_taps, pltpu.roll(edge_taps, 1, 0)], axis=1).astype(BF16)
    step = lane >> 4
    stack = [taps_t[32 * a : 32 * a + 32, 128:256] for a in range(33)]
    column = jnp.concatenate([taps_t[1056:1104, 128:256], jnp.zeros((16, 128), F32)], axis=0)
    step_c = iota((64, 128), 1) >> 4
    none = jnp.zeros((32, 128), F32)
    for shift in (1, 2, 4):
        stack = [
            jnp.where(
                (step & shift) > 0,
                stack[a - shift] if 0 <= a - shift else none,
                stack[a] if a < len(stack) else none,
            )
            for a in range(len(stack) + shift)
        ]
        column = jnp.where((step_c & shift) > 0, pltpu.roll(column, shift, 0), column)
    for a in range(56):
        inside = 8 <= a < 8 + len(stack)
        ws_ref[32 * a : 32 * a + 32, :] = stack[a - 8].astype(BF16) if inside else blank
    wcs_ref[...] = jnp.concatenate([column, pltpu.roll(column, 8, 0)], axis=1).astype(BF16)
    x = iota((128, 128), 0)
    y = iota((128, 128), 1)
    turn = jnp.where(((x >> 5) == (y >> 5)) & ((x & 31) + (y & 31) == 31), 1.0, 0.0).astype(BF16)
    turn_last = jnp.where(
        ((x < 32) & (x + y == 31)) | ((x >= 32) & (x == y)), 1.0, 0.0
    ).astype(BF16)
    turned = [
        jnp.dot(
            taps_f[0:144, 128 * c : 128 * c + 128].astype(BF16),
            turn_last if c == 8 else turn,
            preferred_element_type=F32,
        )
        for c in range(9)
    ]
    lane_w = iota((144, 128), 1)
    final = pltpu.roll(turned[8], 96, 1)
    final = jnp.where(lane_w < 33, final, 0.0)
    turned[8] = jnp.where(lane_w < 32, turned[8], 0.0)
    base = jnp.concatenate(turned, axis=1)
    for w in range(4):
        wf_ref[144 * w : 144 * w + 144, 0:1152] = (
            pltpu.roll(base, 32 * w, 1) if w else base
        ).astype(BF16)
        wf_ref[144 * w : 144 * w + 144, 1152:1280] = (
            pltpu.roll(final, w, 1) if w else final
        ).astype(BF16)

    thr = thrs_ref[...]
    eigs = jnp.concatenate([eig] * 4, axis=0)
    scales = 2.0 * eigs * norm_scale

    def imaged(source, start, ones, tgt, wgt):
        field = jnp.dot(
            wf_ref[:, 0:1024], source[start : start + 1024, :], preferred_element_type=F32
        )
        tail = jnp.concatenate([source[start + 1024 : start + 1152, :], ones], axis=0)
        field += jnp.dot(wf_ref[:, 1024:1200], tail, preferred_element_type=F32)
        power = eigs * (field * field)
        planes = jnp.sum(power.reshape(12, 48, 256), axis=1)
        printed = 1.0 / (1.0 + jnp.exp(-STEEP * (norm_scale * planes - thr)))
        tgt = jnp.concatenate([tgt[v // 3 : v // 3 + 1] for v in range(12)], axis=0)
        wgt = jnp.concatenate([wgt[v // 3 : v // 3 + 1] for v in range(12)], axis=0)
        slopes = wgt * 2.0 * (printed - tgt) * STEEP * printed * (1.0 - printed)
        adjoint = (scales.reshape(12, 48, 1) * slopes[:, None, :]) * field.reshape(12, 48, 256)
        return printed, adjoint.reshape(4, 144, 256).astype(BF16)

    for m in range(8):
        both = [
            jnp.concatenate(
                [tgt_main[kind, 4 * m : 4 * m + 4, :], tgt_main[kind, 4 * m + 32 : 4 * m + 36, :]],
                axis=1,
            )
            for kind in range(2)
        ]
        ones = e_ref[48 * m : 48 * m + 48, :]
        printed, adjoint = imaged(main_t, 128 * m, ones, *both)
        main_a[4 * m : 4 * m + 4] = adjoint[:, :, 0:128]
        main_a[4 * m + 32 : 4 * m + 36] = adjoint[:, :, 128:256]
        for v in range(12):
            w = 4 * m + v // 3
            res_main[v % 3, w : w + 1, :] = printed[v : v + 1, 0:128]
            res_main[v % 3, w + 32 : w + 33, :] = printed[v : v + 1, 128:256]

    for m in range(2):
        both = [tgt_side[kind, 4 * m : 4 * m + 4, :] for kind in range(2)]
        ones = e_ref[48 * (8 + m) : 48 * (9 + m), :]
        printed, adjoint = imaged(side_t, 128 * m, ones, *both)
        side_a[4 * m : 4 * m + 4] = adjoint
        for v in range(12):
            w = 4 * m + v // 3
            res_side[v % 3, w : w + 1, :] = printed[v : v + 1, :]

    for f in range(3):
        edge = jnp.concatenate(
            [res_side[f, :, 32 * g : 32 * g + 16] for g in range(2, 6)], axis=0
        )
        resist_ref[f] = jnp.concatenate([res_main[f, 16:48, 16:128], edge], axis=1)

    d_ref[...] = jnp.zeros_like(d_ref)
    d_last[...] = jnp.zeros_like(d_last)
    for i in (28, 32, *range(0, 28, 4), *range(36, 64, 4)):
        quad = jnp.concatenate(
            [
                jnp.concatenate([main_a[i, 0:128], main_a[i + 2, 0:128]], axis=1),
                jnp.concatenate([main_a[i + 1, 0:128], main_a[i + 3, 0:128]], axis=1),
            ],
            axis=0,
        )
        first, final = max(0, 30 - i), min(33, 63 - i)
        size = 32 * (final + 1 - first)
        left = jnp.concatenate(
            [
                jnp.concatenate(
                    [
                        wt_ref[32 * first + 32 : 32 * first + 32 + size, :],
                        wt_ref[32 * first : 32 * first + size, :],
                    ],
                    axis=1,
                ),
                wc_ref[...],
            ],
            axis=0,
        )
        part = jnp.dot(left, quad, preferred_element_type=F32)
        spot = 32 * (i + first - 30)
        if i == 28:
            h_main[0:1024, :] = part[0:size]
        elif i == 32:
            h_main[64:1024, :] += part[0:960]
            h_main[1024:1088, :] = part[960:1024]
        else:
            h_main[spot : spot + size, :] += part[0:size]
        d_ref[i : i + 48, :] += part[size:]
    for t in range(2):
        rest = jnp.concatenate(
            [
                jnp.concatenate(
                    [main_a[32 * t + r, 128:144], main_a[32 * t + 16 + r, 128:144]], axis=1
                )
                for r in range(16)
            ],
            axis=0,
        )
        first = 16 - 16 * t
        left = jnp.concatenate(
            [
                jnp.concatenate(
                    [
                        ws_ref[32 * first + 256 : 32 * first + 1280, :],
                        ws_ref[32 * first : 32 * first + 1024, :],
                    ],
                    axis=1,
                ),
                wcs_ref[...],
            ],
            axis=0,
        )
        part = jnp.dot(left, rest, preferred_element_type=F32)
        if t == 0:
            h_last[0:1024, :] = part[0:1024]
        else:
            h_last[512:1024, :] += part[0:512]
            h_last[1024:1536, :] = part[512:1024]
        d_last[32 * t : 32 * t + 64, :] += part[1024:]
    rest = jnp.concatenate([side_a[w, 128:144] for w in range(8)], axis=0)
    h_side[...] = jnp.dot(ws_ref[256:1536, :], rest, preferred_element_type=F32)
    for w in range(0, 8, 2):
        pair = jnp.concatenate([side_a[w, 0:128], side_a[w + 1, 0:128]], axis=0)
        left = jnp.concatenate([wt_ref[32:1120, :], wt_ref[0:1088, :]], axis=1)
        h_side[32 * w : 32 * w + 1088, :] += jnp.dot(left, pair, preferred_element_type=F32)

    group = lane >> 5
    for r in range(32):
        body = (
            h_main[32 * r + 64 : 32 * r + 96, 0:128]
            + h_main[32 * r : 32 * r + 32, 128:256]
            + h_last[32 * r + 512 : 32 * r + 544, 0:128]
            + h_last[32 * r : 32 * r + 32, 128:256]
        )
        edge = None
        for half in range(2):
            chosen = None
            for g in range(4 * half, 4 * half + 4):
                u = r + 32 - 8 * g
                if 0 <= u <= 39:
                    term = h_side[32 * u : 32 * u + 32, 128 * half : 128 * half + 128]
                    chosen = jnp.where(group == g % 4, term, 0.0 if chosen is None else chosen)
            edge = chosen if edge is None else edge + chosen
        edge = edge + pltpu.roll(edge, 64, 1)
        edge = edge + pltpu.roll(edge, 32, 1)
        body = pltpu.roll(body, 96, 1, stride=1, stride_axis=0)
        edge = pltpu.roll(edge, 96, 1, stride=1, stride_axis=0)
        both = jnp.where(lane + 32 - tap < 128, body, edge)
        grad_ref[r : r + 1, :] = (
            jnp.sum(both, axis=0, keepdims=True)
            + d_ref[r + 32 : r + 33, 0:128]
            + d_ref[r + 30 : r + 31, 128:256]
            + d_last[r + 32 : r + 33, 0:128]
            + d_last[r + 16 : r + 17, 128:256]
        )


VMEM_SPEC = pl.BlockSpec(memory_space=pltpu.VMEM)


def own_call(*given):
    return pl.pallas_call(
        own_kernel,
        out_shape=(
            jax.ShapeDtypeStruct((1024, 128), BF16),
            jax.ShapeDtypeStruct((256, 256), BF16),
            jax.ShapeDtypeStruct((144, 128), F32),
            jax.ShapeDtypeStruct((12, 256), F32),
        ),
        in_specs=[pl.BlockSpec(memory_space=pl.ANY)] * 3 + [VMEM_SPEC],
        out_specs=(VMEM_SPEC,) * 4,
        scratch_shapes=[
            pltpu.VMEM((8, 128), F32),
            pltpu.VMEM((32, 256), F32),
            pltpu.VMEM((1, 3), F32),
            pltpu.VMEM((1, 72), jnp.int32),
            pltpu.VMEM((1, 72), F32),
            pltpu.SemaphoreType.DMA((3,)),
        ],
        cost_estimate=pl.CostEstimate(flops=2**31, bytes_accessed=2**18, transcendentals=0),
        compiler_params=pltpu.CompilerParams(vmem_limit_bytes=16 * 1024 * 1024),
    )(*given)


def spread_call(*given):
    return pl.pallas_call(
        spread_kernel,
        out_shape=(
            jax.ShapeDtypeStruct((2048, 256), BF16),
            jax.ShapeDtypeStruct((1280, 256), BF16),
            jax.ShapeDtypeStruct((480, 256), BF16),
            jax.ShapeDtypeStruct((2, 64, 128), F32),
            jax.ShapeDtypeStruct((2, 8, 256), F32),
        ),
        in_specs=[VMEM_SPEC] * 6,
        out_specs=(VMEM_SPEC,) * 5,
        scratch_shapes=[
            pltpu.VMEM((112, 256), F32),
            pltpu.VMEM((56, 256), F32),
            pltpu.VMEM((56, 256), F32),
            pltpu.VMEM((32, 352), F32),
            pltpu.VMEM((32, 352), F32),
        ],
        cost_estimate=pl.CostEstimate(flops=2**29, bytes_accessed=2**21, transcendentals=0),
        compiler_params=pltpu.CompilerParams(vmem_limit_bytes=16 * 1024 * 1024),
    )(*given)


def step_call(spread, order, four, other):
    return pl.pallas_call(
        step_kernel,
        out_shape=(
            jax.ShapeDtypeStruct((32, 128), F32),
            jax.ShapeDtypeStruct((3, 32, 128), F32),
        ),
        in_specs=[VMEM_SPEC] * 10,
        out_specs=(VMEM_SPEC, VMEM_SPEC),
        scratch_shapes=[
            pltpu.VMEM((256, 1152), BF16),
            pltpu.VMEM((576, 1280), BF16),
            pltpu.VMEM((1120, 128), BF16),
            pltpu.VMEM((48, 256), BF16),
            pltpu.VMEM((1792, 128), BF16),
            pltpu.VMEM((64, 256), BF16),
            pltpu.VMEM((64, 144, 128), BF16),
            pltpu.VMEM((8, 144, 256), BF16),
            pltpu.VMEM((1088, 256), F32),
            pltpu.VMEM((1536, 256), F32),
            pltpu.VMEM((1280, 256), F32),
            pltpu.VMEM((112, 256), F32),
            pltpu.VMEM((96, 256), F32),
            pltpu.VMEM((3, 64, 128), F32),
            pltpu.VMEM((3, 8, 256), F32),
        ],
        compiler_params=pltpu.CompilerParams(vmem_limit_bytes=32 * 1024 * 1024),
    )(*spread, *order, four, other)


def flat_taps(kernels):
    count = kernels.shape[0] * 2
    pairs = kernels.reshape(count, 33, 33)
    return jnp.concatenate(
        [
            pairs[:, :, :32].reshape(count, 1056),
            pairs[:, :, 32],
            jnp.zeros((count, 63), BF16),
        ],
        axis=1,
    )


def on_device(mask, kernels, eigen, focus, target, pixel_weight, threshold):
    strips = lax.axis_size("strip")
    me = lax.axis_index("kern")

    odd = lax.axis_index("strip") % 2

    def columns(array, rim, row=0, count=32):
        wide = jnp.pad(array.astype(F32), ((0, 0), (rim, rim)))
        return lax.dynamic_slice(wide, (row, me * 128), (count, 128 + 2 * rim))

    def rim_rows(row):
        edges = [columns(target, 16, row, 16), columns(pixel_weight, 16, row, 16)]
        return jnp.concatenate([columns(mask, 32), jnp.concatenate(edges, axis=0)], axis=1)

    near_pairs = [(i, i ^ 1) for i in range(strips)]
    far_pairs = [((i + 1) % strips, ((i ^ 1) + 1) % strips) for i in range(strips)]
    near = lax.ppermute(rim_rows(16 - 16 * odd), "strip", near_pairs)
    far = lax.ppermute(rim_rows(16 * odd), "strip", far_pairs)

    taps = flat_taps(kernels)
    four = jnp.stack(
        [taps]
        + [lax.ppermute(taps, "kern", [(i, i ^ (2 * s)) for i in range(8)]) for s in range(1, 4)]
    )
    other = lax.ppermute(four, "kern", [(i, i ^ 1) for i in range(8)])

    own_mask = columns(mask, 32)
    center, *order = own_call(
        threshold.reshape(1, 3), focus.reshape(1, 72), eigen.reshape(1, 72), own_mask
    )
    spread = spread_call(
        center, own_mask, columns(target, 16), columns(pixel_weight, 16), near, far
    )
    return step_call(spread, order, four, other)


def solution(mesh):
    placed = (
        P("strip", None),
        P("kern", None, None, None),
        P(),
        P(),
        P("strip", None),
        P("strip", None),
        P(),
    )
    return jax.shard_map(
        on_device,
        mesh=mesh,
        in_specs=placed,
        out_specs=(P("strip", "kern"), P(None, "strip", "kern")),
        check_vma=False,
    )
```

```python
import jax
import jax.numpy as jnp
from jax import lax
from jax.experimental import pallas as pl
from jax.experimental.pallas import tpu as pltpu
from jax.sharding import PartitionSpec as P

STEEP = 20.0
F32 = jnp.float32
BF16 = jnp.bfloat16


def iota(shape, dim):
    return lax.broadcasted_iota(jnp.int32, shape, dim)


def skewed(eight, j, tap, lane):
    left = jnp.broadcast_to(eight[j : j + 1, 0:128], (32, 128))
    right = jnp.broadcast_to(eight[j : j + 1, 128:256], (32, 128))
    left = pltpu.roll(left, 97, 1, stride=1, stride_axis=0)
    right = pltpu.roll(right, 97, 1, stride=1, stride_axis=0)
    return jnp.where(lane + 31 - tap < 128, left, right).astype(BF16)


def own_kernel(
    thr_ref, focus_ref, eigen_ref, mask_ref,
    center, pick_ref, eig_ref, thrs_ref,
    both_ref, rows_ref, thr_vm, focus_vm, eigen_vm, sems,
):
    me = lax.axis_index("kern")
    copies = [
        pltpu.make_async_copy(src, dst, sems.at[n])
        for n, (src, dst) in enumerate(
            ((thr_ref, thr_vm), (focus_ref, focus_vm), (eigen_ref, eigen_vm))
        )
    ]
    for copy in copies:
        copy.start()
    rows_ref[:, 128:256] = jnp.zeros((32, 128), F32)
    rows_ref[:, 0:192] = mask_ref[...]
    tap = iota((32, 128), 0)
    lane = iota((32, 128), 1)

    def spread_own(block, _):
        eight = rows_ref[pl.ds(pl.multiple_of(block * 8, 8), 8), :]
        for j in range(8):
            spot = pl.multiple_of((block * 8 + j) * 32, 32)
            center[pl.ds(spot, 32), :] = skewed(eight, j, tap, lane)
        return 0

    lax.fori_loop(0, 4, spread_own, 0)

    for copy in copies:
        copy.wait()
    both_ref[...] = jnp.zeros((8, 128), F32)
    both_ref[0:1, 0:72] = focus_vm[...].astype(F32)
    both_ref[1:2, 0:72] = eigen_vm[...]
    listed = jnp.transpose(both_ref[...])
    slot = iota((1, 256), 1)
    place = slot & 127
    block = (place >= 18).astype(jnp.int32) + (place >= 36) + (place >= 54)
    holder = me ^ (2 * block + (slot >> 7))
    inside = place < 72
    system = jnp.where(inside, 9 * holder + ((place - 18 * block) >> 1), -1)
    here = iota((128, 256), 0) == system
    frow = jnp.sum(jnp.where(here, listed[:, 0:1], 0.0), axis=0, keepdims=True)
    frow = jnp.where(inside, frow, -1.0)
    erow = jnp.sum(jnp.where(here, listed[:, 1:2], 0.0), axis=0, keepdims=True)
    fcol = jnp.transpose(jnp.broadcast_to(frow, (8, 256)))[:, 0:1]
    before = (fcol == frow) & (iota((256, 256), 0) < iota((256, 256), 1))
    rank = jnp.sum(jnp.where(before, 1.0, 0.0), axis=0, keepdims=True)
    pos = jnp.where(frow >= 0.0, frow * 48.0 + rank, -1.0)
    spot = iota((256, 256), 0)
    spot = jnp.where(spot < 128, spot, 128 + (spot & 15))
    pick = jnp.where(spot.astype(F32) == pos, 1.0, 0.0)
    pick_ref[...] = pick.astype(BF16)
    eig = jnp.sum(pick * erow, axis=1, keepdims=True)[0:144]
    eig_ref[...] = jnp.broadcast_to(eig, (144, 128))
    for v in range(12):
        thrs_ref[v : v + 1, :] = jnp.broadcast_to(thr_vm[0:1, v % 3 : v % 3 + 1], (1, 256))


def spread_kernel(
    center, mask_ref, target_ref, weight_ref, near_ref, far_ref,
    main_t, side_t, e_ref, tgt_main, tgt_side,
    rows_ref, lo_ref, hi_ref, up_ref, down_ref,
):
    strip = lax.axis_index("strip")
    last = lax.axis_size("strip") - 1

    odd = jnp.full((32, 352), strip & 1, jnp.int32) > 0
    up_ref[...] = jnp.where(odd, near_ref[...], far_ref[...])
    down_ref[...] = jnp.where(odd, far_ref[...], near_ref[...])

    has_up = (strip > 0).astype(F32)
    has_down = (strip < last).astype(F32)
    rows_ref[96:, :] = jnp.zeros((16, 256), F32)
    rows_ref[:, 128:] = jnp.zeros((112, 128), F32)
    rows_ref[0:32, 0:192] = up_ref[:, 0:192] * has_up
    rows_ref[32:64, 0:192] = mask_ref[...]
    rows_ref[64:96, 0:192] = down_ref[:, 0:192] * has_down

    for kind in range(2):
        above = up_ref[16 * kind : 16 * kind + 16, 192:352]
        below = down_ref[16 * kind : 16 * kind + 16, 192:352]
        if kind == 1:
            above = above * has_up
            below = below * has_down
        mine = (weight_ref if kind else target_ref)[...]
        area = jnp.concatenate([above, mine, below], axis=0)
        tgt_main[kind] = area[:, 0:128]
        tgt_side[kind] = jnp.concatenate(
            [area[8 * g : 8 * g + 8, 128:160] for g in range(8)], axis=1
        )

    lo_ref[...] = jnp.concatenate([rows_ref[8 * g : 8 * g + 56, 128:160] for g in range(8)], axis=1)
    hi_ref[...] = jnp.concatenate([rows_ref[8 * g : 8 * g + 56, 160:192] for g in range(8)], axis=1)

    tap = iota((32, 128), 0)
    lane = iota((32, 128), 1)

    main_t[1024:2048, 0:128] = center[...]
    main_t[0:1024, 128:256] = center[...]

    def spread_rim(block, _):
        start = pl.multiple_of(block * 8, 8)
        above, below = rows_ref[pl.ds(start, 8), :], rows_ref[pl.ds(start + 64, 8), :]
        for j in range(8):
            spot = pl.multiple_of((block * 8 + j) * 32, 32)
            main_t[pl.ds(spot, 32), 0:128] = skewed(above, j, tap, lane)
            main_t[pl.ds(spot + 1024, 32), 128:256] = skewed(below, j, tap, lane)
        return 0

    lax.fori_loop(0, 4, spread_rim, 0)

    def spread_side(block, _):
        start = pl.multiple_of(block * 8, 8)
        lows, highs = lo_ref[pl.ds(start, 8), :], hi_ref[pl.ds(start, 8), :]
        for j in range(8):
            for half in range(2):
                cols = slice(128 * half, 128 * half + 128)
                low = jnp.broadcast_to(lows[j : j + 1, cols], (32, 128))
                high = jnp.broadcast_to(highs[j : j + 1, cols], (32, 128))
                low = pltpu.roll(low, 97, 1, stride=1, stride_axis=0)
                high = pltpu.roll(high, 1, 1, stride=1, stride_axis=0)
                both = jnp.where((lane & 31) <= tap, low, high).astype(BF16)
                side_t[pl.ds(pl.multiple_of((block * 8 + j) * 32, 32), 32), cols] = both
        return 0

    lax.fori_loop(0, 5, spread_side, 0)

    for m in range(8):
        e_ref[48 * m : 48 * m + 48, :] = jnp.concatenate(
            [rows_ref[4 * m : 4 * m + 48, 32:160], rows_ref[4 * m + 32 : 4 * m + 80, 32:160]], axis=1
        ).astype(BF16)
    for m in range(2):
        e_ref[48 * (8 + m) : 48 * (9 + m), :] = hi_ref[4 * m : 4 * m + 48, :].astype(BF16)


def step_kernel(
    main_t, side_t, e_ref, tgt_main, tgt_side, pick_ref, eig_ref, thrs_ref, four_ref, other_ref,
    grad_ref, resist_ref,
    raw_ref, wf_ref, wt_ref, wc_ref, ws_ref, wcs_ref, main_a, side_a,
    h_main, h_last, h_side, d_ref, d_last, res_main, res_side,
):
    norm_scale = 3.0 / 72
    tap = iota((32, 128), 0)
    lane = iota((32, 128), 1)
    eig = eig_ref[:, 0:1]

    raw_ref[...] = jnp.zeros_like(raw_ref)
    raw_ref[0:72, :] = four_ref[...]
    raw_ref[128:200, :] = other_ref[...]
    taps_f = jnp.dot(pick_ref[...], raw_ref[...], preferred_element_type=F32)
    taps_t = jnp.transpose(taps_f)
    blank = jnp.zeros((32, 128), BF16)
    wt_ref[0:32, :] = blank
    wt_ref[32:1088, :] = taps_t[0:1056, 0:128].astype(BF16)
    wt_ref[1088:1120, :] = blank
    edge_taps = taps_t[1056:1104, 0:128]
    wc_ref[...] = jnp.concatenate([edge_taps, pltpu.roll(edge_taps, 1, 0)], axis=1).astype(BF16)
    step = lane >> 4
    stack = [taps_t[32 * a : 32 * a + 32, 128:256] for a in range(33)]
    column = jnp.concatenate([taps_t[1056:1104, 128:256], jnp.zeros((16, 128), F32)], axis=0)
    step_c = iota((64, 128), 1) >> 4
    none = jnp.zeros((32, 128), F32)
    for shift in (1, 2, 4):
        stack = [
            jnp.where(
                (step & shift) > 0,
                stack[a - shift] if 0 <= a - shift else none,
                stack[a] if a < len(stack) else none,
            )
            for a in range(len(stack) + shift)
        ]
        column = jnp.where((step_c & shift) > 0, pltpu.roll(column, shift, 0), column)
    for a in range(56):
        inside = 8 <= a < 8 + len(stack)
        ws_ref[32 * a : 32 * a + 32, :] = stack[a - 8].astype(BF16) if inside else blank
    wcs_ref[...] = jnp.concatenate([column, pltpu.roll(column, 8, 0)], axis=1).astype(BF16)
    x = iota((128, 128), 0)
    y = iota((128, 128), 1)
    turn = jnp.where(((x >> 5) == (y >> 5)) & ((x & 31) + (y & 31) == 31), 1.0, 0.0).astype(BF16)
    turn_last = jnp.where(
        ((x < 32) & (x + y == 31)) | ((x >= 32) & (x == y)), 1.0, 0.0
    ).astype(BF16)
    turned = [
        jnp.dot(
            taps_f[0:144, 128 * c : 128 * c + 128].astype(BF16),
            turn_last if c == 8 else turn,
            preferred_element_type=F32,
        )
        for c in range(9)
    ]
    lane_w = iota((144, 128), 1)
    final = pltpu.roll(turned[8], 96, 1)
    final = jnp.where(lane_w < 33, final, 0.0)
    turned[8] = jnp.where(lane_w < 32, turned[8], 0.0)
    base = jnp.concatenate(turned, axis=1)
    for w in range(4):
        wf_ref[144 * w : 144 * w + 144, 0:1152] = (
            pltpu.roll(base, 32 * w, 1) if w else base
        ).astype(BF16)
        wf_ref[144 * w : 144 * w + 144, 1152:1280] = (
            pltpu.roll(final, w, 1) if w else final
        ).astype(BF16)

    thr = thrs_ref[...]
    eigs = jnp.concatenate([eig] * 4, axis=0)
    scales = 2.0 * eigs * norm_scale

    def imaged(source, start, ones, tgt, wgt):
        field = jnp.dot(
            wf_ref[:, 0:1024], source[start : start + 1024, :], preferred_element_type=F32
        )
        tail = jnp.concatenate([source[start + 1024 : start + 1152, :], ones], axis=0)
        field += jnp.dot(wf_ref[:, 1024:1200], tail, preferred_element_type=F32)
        power = eigs * (field * field)
        planes = jnp.sum(power.reshape(12, 48, 256), axis=1)
        printed = 1.0 / (1.0 + jnp.exp(-STEEP * (norm_scale * planes - thr)))
        tgt = jnp.concatenate([tgt[v // 3 : v // 3 + 1] for v in range(12)], axis=0)
        wgt = jnp.concatenate([wgt[v // 3 : v // 3 + 1] for v in range(12)], axis=0)
        slopes = wgt * 2.0 * (printed - tgt) * STEEP * printed * (1.0 - printed)
        adjoint = (scales.reshape(12, 48, 1) * slopes[:, None, :]) * field.reshape(12, 48, 256)
        return printed, adjoint.reshape(4, 144, 256).astype(BF16)

    for m in range(8):
        both = [
            jnp.concatenate(
                [tgt_main[kind, 4 * m : 4 * m + 4, :], tgt_main[kind, 4 * m + 32 : 4 * m + 36, :]],
                axis=1,
            )
            for kind in range(2)
        ]
        ones = e_ref[48 * m : 48 * m + 48, :]
        printed, adjoint = imaged(main_t, 128 * m, ones, *both)
        main_a[4 * m : 4 * m + 4] = adjoint[:, :, 0:128]
        main_a[4 * m + 32 : 4 * m + 36] = adjoint[:, :, 128:256]
        for v in range(12):
            w = 4 * m + v // 3
            res_main[v % 3, w : w + 1, :] = printed[v : v + 1, 0:128]
            res_main[v % 3, w + 32 : w + 33, :] = printed[v : v + 1, 128:256]

    for m in range(2):
        both = [tgt_side[kind, 4 * m : 4 * m + 4, :] for kind in range(2)]
        ones = e_ref[48 * (8 + m) : 48 * (9 + m), :]
        printed, adjoint = imaged(side_t, 128 * m, ones, *both)
        side_a[4 * m : 4 * m + 4] = adjoint
        for v in range(12):
            w = 4 * m + v // 3
            res_side[v % 3, w : w + 1, :] = printed[v : v + 1, :]

    for f in range(3):
        edge = jnp.concatenate(
            [res_side[f, :, 32 * g : 32 * g + 16] for g in range(2, 6)], axis=0
        )
        resist_ref[f] = jnp.concatenate([res_main[f, 16:48, 16:128], edge], axis=1)

    d_ref[...] = jnp.zeros_like(d_ref)
    d_last[...] = jnp.zeros_like(d_last)
    for i in (28, 32, *range(0, 28, 4), *range(36, 64, 4)):
        quad = jnp.concatenate(
            [
                jnp.concatenate([main_a[i, 0:128], main_a[i + 2, 0:128]], axis=1),
                jnp.concatenate([main_a[i + 1, 0:128], main_a[i + 3, 0:128]], axis=1),
            ],
            axis=0,
        )
        first, final = max(0, 30 - i), min(33, 63 - i)
        size = 32 * (final + 1 - first)
        left = jnp.concatenate(
            [
                jnp.concatenate(
                    [
                        wt_ref[32 * first + 32 : 32 * first + 32 + size, :],
                        wt_ref[32 * first : 32 * first + size, :],
                    ],
                    axis=1,
                ),
                wc_ref[...],
            ],
            axis=0,
        )
        part = jnp.dot(left, quad, preferred_element_type=F32)
        spot = 32 * (i + first - 30)
        if i == 28:
            h_main[0:1024, :] = part[0:size]
        elif i == 32:
            h_main[64:1024, :] += part[0:960]
            h_main[1024:1088, :] = part[960:1024]
        else:
            h_main[spot : spot + size, :] += part[0:size]
        d_ref[i : i + 48, :] += part[size:]
    for t in range(2):
        rest = jnp.concatenate(
            [
                jnp.concatenate(
                    [main_a[32 * t + r, 128:144], main_a[32 * t + 16 + r, 128:144]], axis=1
                )
                for r in range(16)
            ],
            axis=0,
        )
        first = 16 - 16 * t
        left = jnp.concatenate(
            [
                jnp.concatenate(
                    [
                        ws_ref[32 * first + 256 : 32 * first + 1280, :],
                        ws_ref[32 * first : 32 * first + 1024, :],
                    ],
                    axis=1,
                ),
                wcs_ref[...],
            ],
            axis=0,
        )
        part = jnp.dot(left, rest, preferred_element_type=F32)
        if t == 0:
            h_last[0:1024, :] = part[0:1024]
        else:
            h_last[512:1024, :] += part[0:512]
            h_last[1024:1536, :] = part[512:1024]
        d_last[32 * t : 32 * t + 64, :] += part[1024:]
    rest = jnp.concatenate([side_a[w, 128:144] for w in range(8)], axis=0)
    h_side[...] = jnp.dot(ws_ref[256:1536, :], rest, preferred_element_type=F32)
    for w in range(0, 8, 2):
        pair = jnp.concatenate([side_a[w, 0:128], side_a[w + 1, 0:128]], axis=0)
        left = jnp.concatenate([wt_ref[32:1120, :], wt_ref[0:1088, :]], axis=1)
        h_side[32 * w : 32 * w + 1088, :] += jnp.dot(left, pair, preferred_element_type=F32)

    group = lane >> 5
    for r in range(32):
        body = (
            h_main[32 * r + 64 : 32 * r + 96, 0:128]
            + h_main[32 * r : 32 * r + 32, 128:256]
            + h_last[32 * r + 512 : 32 * r + 544, 0:128]
            + h_last[32 * r : 32 * r + 32, 128:256]
        )
        edge = None
        for half in range(2):
            chosen = None
            for g in range(4 * half, 4 * half + 4):
                u = r + 32 - 8 * g
                if 0 <= u <= 39:
                    term = h_side[32 * u : 32 * u + 32, 128 * half : 128 * half + 128]
                    chosen = jnp.where(group == g % 4, term, 0.0 if chosen is None else chosen)
            edge = chosen if edge is None else edge + chosen
        edge = edge + pltpu.roll(edge, 64, 1)
        edge = edge + pltpu.roll(edge, 32, 1)
        body = pltpu.roll(body, 96, 1, stride=1, stride_axis=0)
        edge = pltpu.roll(edge, 96, 1, stride=1, stride_axis=0)
        both = jnp.where(lane + 32 - tap < 128, body, edge)
        grad_ref[r : r + 1, :] = (
            jnp.sum(both, axis=0, keepdims=True)
            + d_ref[r + 32 : r + 33, 0:128]
            + d_ref[r + 30 : r + 31, 128:256]
            + d_last[r + 32 : r + 33, 0:128]
            + d_last[r + 16 : r + 17, 128:256]
        )


VMEM_SPEC = pl.BlockSpec(memory_space=pltpu.VMEM)


def own_call(*given):
    return pl.pallas_call(
        own_kernel,
        out_shape=(
            jax.ShapeDtypeStruct((1024, 128), BF16),
            jax.ShapeDtypeStruct((256, 256), BF16),
            jax.ShapeDtypeStruct((144, 128), F32),
            jax.ShapeDtypeStruct((12, 256), F32),
        ),
        in_specs=[pl.BlockSpec(memory_space=pl.ANY)] * 3 + [VMEM_SPEC],
        out_specs=(VMEM_SPEC,) * 4,
        scratch_shapes=[
            pltpu.VMEM((8, 128), F32),
            pltpu.VMEM((32, 256), F32),
            pltpu.VMEM((1, 3), F32),
            pltpu.VMEM((1, 72), jnp.int32),
            pltpu.VMEM((1, 72), F32),
            pltpu.SemaphoreType.DMA((3,)),
        ],
        cost_estimate=pl.CostEstimate(flops=2**31, bytes_accessed=2**18, transcendentals=0),
        compiler_params=pltpu.CompilerParams(vmem_limit_bytes=16 * 1024 * 1024),
    )(*given)


def spread_call(*given):
    return pl.pallas_call(
        spread_kernel,
        out_shape=(
            jax.ShapeDtypeStruct((2048, 256), BF16),
            jax.ShapeDtypeStruct((1280, 256), BF16),
            jax.ShapeDtypeStruct((480, 256), BF16),
            jax.ShapeDtypeStruct((2, 64, 128), F32),
            jax.ShapeDtypeStruct((2, 8, 256), F32),
        ),
        in_specs=[VMEM_SPEC] * 6,
        out_specs=(VMEM_SPEC,) * 5,
        scratch_shapes=[
            pltpu.VMEM((112, 256), F32),
            pltpu.VMEM((56, 256), F32),
            pltpu.VMEM((56, 256), F32),
            pltpu.VMEM((32, 352), F32),
            pltpu.VMEM((32, 352), F32),
        ],
        cost_estimate=pl.CostEstimate(flops=2**29, bytes_accessed=2**21, transcendentals=0),
        compiler_params=pltpu.CompilerParams(vmem_limit_bytes=16 * 1024 * 1024),
    )(*given)


def step_call(spread, order, four, other):
    return pl.pallas_call(
        step_kernel,
        out_shape=(
            jax.ShapeDtypeStruct((32, 128), F32),
            jax.ShapeDtypeStruct((3, 32, 128), F32),
        ),
        in_specs=[VMEM_SPEC] * 10,
        out_specs=(VMEM_SPEC, VMEM_SPEC),
        scratch_shapes=[
            pltpu.VMEM((256, 1152), BF16),
            pltpu.VMEM((576, 1280), BF16),
            pltpu.VMEM((1120, 128), BF16),
            pltpu.VMEM((48, 256), BF16),
            pltpu.VMEM((1792, 128), BF16),
            pltpu.VMEM((64, 256), BF16),
            pltpu.VMEM((64, 144, 128), BF16),
            pltpu.VMEM((8, 144, 256), BF16),
            pltpu.VMEM((1088, 256), F32),
            pltpu.VMEM((1536, 256), F32),
            pltpu.VMEM((1280, 256), F32),
            pltpu.VMEM((112, 256), F32),
            pltpu.VMEM((96, 256), F32),
            pltpu.VMEM((3, 64, 128), F32),
            pltpu.VMEM((3, 8, 256), F32),
        ],
        compiler_params=pltpu.CompilerParams(vmem_limit_bytes=32 * 1024 * 1024),
    )(*spread, *order, four, other)


def flat_taps(kernels):
    count = kernels.shape[0] * 2
    pairs = kernels.reshape(count, 33, 33)
    return jnp.concatenate(
        [
            pairs[:, :, :32].reshape(count, 1056),
            pairs[:, :, 32],
            jnp.zeros((count, 63), BF16),
        ],
        axis=1,
    )


def on_device(mask, kernels, eigen, focus, target, pixel_weight, threshold):
    strips = lax.axis_size("strip")
    me = lax.axis_index("kern")

    odd = lax.axis_index("strip") % 2

    def columns(array, rim, row=0, count=32):
        wide = jnp.pad(array.astype(F32), ((0, 0), (rim, rim)))
        return lax.dynamic_slice(wide, (row, me * 128), (count, 128 + 2 * rim))

    def rim_rows(row):
        edges = [columns(target, 16, row, 16), columns(pixel_weight, 16, row, 16)]
        return jnp.concatenate([columns(mask, 32), jnp.concatenate(edges, axis=0)], axis=1)

    near_pairs = [(i, i ^ 1) for i in range(strips)]
    far_pairs = []
    for k in range(8):
        for i in range(strips):
            if i in (0, strips - 1):
                far_pairs.append((k * strips + i, (k ^ 1) * strips + i))
            else:
                far_pairs.append((k * strips + i, k * strips + ((i - 1) ^ 1) + 1))
    near = lax.ppermute(rim_rows(16 - 16 * odd), "strip", near_pairs)
    far = lax.ppermute(rim_rows(16 * odd), ("kern", "strip"), far_pairs)

    taps = flat_taps(kernels)
    four = jnp.concatenate(
        [taps]
        + [lax.ppermute(taps, "kern", [(i, i ^ (2 * s)) for i in range(8)]) for s in range(1, 4)]
    )
    beside = [
        (k * strips + s, (k ^ 1) * strips + (s ^ (strips // 2) if s % 2 else s))
        for k in range(8)
        for s in range(strips)
    ]
    other = lax.ppermute(four, ("kern", "strip"), beside)

    own_mask = columns(mask, 32)
    center, *order = own_call(
        threshold.reshape(1, 3), focus.reshape(1, 72), eigen.reshape(1, 72), own_mask
    )
    spread = spread_call(
        center, own_mask, columns(target, 16), columns(pixel_weight, 16), near, far
    )
    return step_call(spread, order, four, other)


def solution(mesh):
    placed = (
        P("strip", None),
        P("kern", None, None, None),
        P(),
        P(),
        P("strip", None),
        P("strip", None),
        P(),
    )
    return jax.shard_map(
        on_device,
        mesh=mesh,
        in_specs=placed,
        out_specs=(P("strip", "kern"), P(None, "strip", "kern")),
        check_vma=False,
    )
```

```python
import jax
import jax.numpy as jnp
from jax import lax
from jax.experimental import pallas as pl
from jax.experimental.pallas import tpu as pltpu
from jax.sharding import PartitionSpec as P

STEEP = 20.0
F32 = jnp.float32
BF16 = jnp.bfloat16


def iota(shape, dim):
    return lax.broadcasted_iota(jnp.int32, shape, dim)


def skewed(eight, j, tap, lane):
    left = jnp.broadcast_to(eight[j : j + 1, 0:128], (32, 128))
    right = jnp.broadcast_to(eight[j : j + 1, 128:256], (32, 128))
    both = jnp.where(lane < 31 - tap, right, left)
    return pltpu.roll(both, 97, 1, stride=1, stride_axis=0).astype(BF16)


def own_kernel(
    thr_ref, focus_ref, eigen_ref, mask_ref,
    center, pick_ref, eig_ref, thrs_ref,
    both_ref, rows_ref, thr_vm, focus_vm, eigen_vm, sems,
):
    me = lax.axis_index("kern")
    copies = [
        pltpu.make_async_copy(src, dst, sems.at[n])
        for n, (src, dst) in enumerate(
            ((thr_ref, thr_vm), (focus_ref, focus_vm), (eigen_ref, eigen_vm))
        )
    ]
    for copy in copies:
        copy.start()
    rows_ref[:, 128:256] = jnp.zeros((32, 128), F32)
    rows_ref[:, 0:192] = mask_ref[...]
    tap = iota((32, 128), 0)
    lane = iota((32, 128), 1)

    def spread_own(block, _):
        eight = rows_ref[pl.ds(pl.multiple_of(block * 8, 8), 8), :]
        for j in range(8):
            spot = pl.multiple_of((block * 8 + j) * 32, 32)
            center[pl.ds(spot, 32), :] = skewed(eight, j, tap, lane)
        return 0

    lax.fori_loop(0, 4, spread_own, 0)

    for copy in copies:
        copy.wait()
    both_ref[...] = jnp.zeros((8, 128), F32)
    both_ref[0:1, 0:72] = focus_vm[...].astype(F32)
    both_ref[1:2, 0:72] = eigen_vm[...]
    listed = jnp.transpose(both_ref[...])
    slot = iota((1, 256), 1)
    place = slot & 127
    block = (place >= 18).astype(jnp.int32) + (place >= 36) + (place >= 54)
    holder = me ^ (2 * block + (slot >> 7))
    inside = place < 72
    system = jnp.where(inside, 9 * holder + ((place - 18 * block) >> 1), -1)
    here = iota((128, 256), 0) == system
    frow = jnp.sum(jnp.where(here, listed[:, 0:1], 0.0), axis=0, keepdims=True)
    frow = jnp.where(inside, frow, -1.0)
    erow = jnp.sum(jnp.where(here, listed[:, 1:2], 0.0), axis=0, keepdims=True)
    fcol = jnp.transpose(jnp.broadcast_to(frow, (8, 256)))[:, 0:1]
    before = (fcol == frow) & (iota((256, 256), 0) < iota((256, 256), 1))
    rank = jnp.sum(jnp.where(before, 1.0, 0.0), axis=0, keepdims=True)
    pos = jnp.where(frow >= 0.0, frow * 48.0 + rank, -1.0)
    spot = iota((256, 256), 0)
    spot = jnp.where(spot < 128, spot, 128 + (spot & 15))
    pick = jnp.where(spot.astype(F32) == pos, 1.0, 0.0)
    pick_ref[...] = pick.astype(BF16)
    eig = jnp.sum(pick * erow, axis=1, keepdims=True)[0:144]
    eig_ref[...] = jnp.broadcast_to(eig, (144, 128))
    for v in range(12):
        thrs_ref[v : v + 1, :] = jnp.broadcast_to(thr_vm[0:1, v % 3 : v % 3 + 1], (1, 256))


def spread_kernel(
    center, mask_ref, target_ref, weight_ref, near_ref, far_ref,
    main_t, side_t, e_ref, tgt_main, tgt_side,
    rows_ref, lo_ref, hi_ref, up_ref, down_ref,
):
    strip = lax.axis_index("strip")
    last = lax.axis_size("strip") - 1

    odd = jnp.full((32, 352), strip & 1, jnp.int32) > 0
    up_ref[...] = jnp.where(odd, near_ref[...], far_ref[...])
    down_ref[...] = jnp.where(odd, far_ref[...], near_ref[...])

    has_up = (strip > 0).astype(F32)
    has_down = (strip < last).astype(F32)
    rows_ref[96:, :] = jnp.zeros((16, 256), F32)
    rows_ref[:, 128:] = jnp.zeros((112, 128), F32)
    rows_ref[0:32, 0:192] = up_ref[:, 0:192] * has_up
    rows_ref[32:64, 0:192] = mask_ref[...]
    rows_ref[64:96, 0:192] = down_ref[:, 0:192] * has_down

    for kind in range(2):
        above = up_ref[16 * kind : 16 * kind + 16, 192:352]
        below = down_ref[16 * kind : 16 * kind + 16, 192:352]
        if kind == 1:
            above = above * has_up
            below = below * has_down
        mine = (weight_ref if kind else target_ref)[...]
        area = jnp.concatenate([above, mine, below], axis=0)
        tgt_main[kind] = area[:, 0:128]
        tgt_side[kind] = jnp.concatenate(
            [area[8 * g : 8 * g + 8, 128:160] for g in range(8)], axis=1
        )

    lo_ref[...] = jnp.concatenate([rows_ref[8 * g : 8 * g + 56, 128:160] for g in range(8)], axis=1)
    hi_ref[...] = jnp.concatenate([rows_ref[8 * g : 8 * g + 56, 160:192] for g in range(8)], axis=1)

    tap = iota((32, 128), 0)
    lane = iota((32, 128), 1)

    main_t[1024:2048, 0:128] = center[...]
    main_t[0:1024, 128:256] = center[...]

    def spread_rim(block, _):
        start = pl.multiple_of(block * 8, 8)
        above, below = rows_ref[pl.ds(start, 8), :], rows_ref[pl.ds(start + 64, 8), :]
        for j in range(8):
            spot = pl.multiple_of((block * 8 + j) * 32, 32)
            main_t[pl.ds(spot, 32), 0:128] = skewed(above, j, tap, lane)
            main_t[pl.ds(spot + 1024, 32), 128:256] = skewed(below, j, tap, lane)
        return 0

    lax.fori_loop(0, 4, spread_rim, 0)

    def spread_side(block, _):
        start = pl.multiple_of(block * 8, 8)
        lows, highs = lo_ref[pl.ds(start, 8), :], hi_ref[pl.ds(start, 8), :]
        turned = [pltpu.roll(highs[:, 128 * h : 128 * h + 128], 32, 1) for h in range(2)]
        for j in range(8):
            for half in range(2):
                cols = slice(128 * half, 128 * half + 128)
                low = jnp.broadcast_to(lows[j : j + 1, cols], (32, 128))
                high = jnp.broadcast_to(turned[half][j : j + 1], (32, 128))
                both = jnp.where((lane & 31) >= 31 - tap, low, high)
                both = pltpu.roll(both, 97, 1, stride=1, stride_axis=0).astype(BF16)
                side_t[pl.ds(pl.multiple_of((block * 8 + j) * 32, 32), 32), cols] = both
        return 0

    lax.fori_loop(0, 5, spread_side, 0)

    for m in range(8):
        e_ref[48 * m : 48 * m + 48, :] = jnp.concatenate(
            [rows_ref[4 * m : 4 * m + 48, 32:160], rows_ref[4 * m + 32 : 4 * m + 80, 32:160]], axis=1
        ).astype(BF16)
    for m in range(2):
        e_ref[48 * (8 + m) : 48 * (9 + m), :] = hi_ref[4 * m : 4 * m + 48, :].astype(BF16)


def step_kernel(
    main_t, side_t, e_ref, tgt_main, tgt_side, pick_ref, eig_ref, thrs_ref, four_ref, other_ref,
    grad_ref, resist_ref,
    raw_ref, wf_ref, wt_ref, wc_ref, ws_ref, wcs_ref, main_a, side_a,
    h_main, h_last, h_side, d_ref, d_last, res_main, res_side,
):
    norm_scale = 3.0 / 72
    tap = iota((32, 128), 0)
    lane = iota((32, 128), 1)
    eig = eig_ref[:, 0:1]

    raw_ref[...] = jnp.zeros_like(raw_ref)
    raw_ref[0:72, :] = four_ref[...]
    raw_ref[128:200, :] = other_ref[...]
    taps_f = jnp.dot(pick_ref[...], raw_ref[...], preferred_element_type=F32)
    taps_t = jnp.transpose(taps_f)
    blank = jnp.zeros((32, 128), BF16)
    wt_ref[0:32, :] = blank
    wt_ref[32:1088, :] = taps_t[0:1056, 0:128].astype(BF16)
    wt_ref[1088:1120, :] = blank
    edge_taps = taps_t[1056:1104, 0:128]
    wc_ref[...] = jnp.concatenate([edge_taps, pltpu.roll(edge_taps, 1, 0)], axis=1).astype(BF16)
    step = lane >> 4
    stack = [taps_t[32 * a : 32 * a + 32, 128:256] for a in range(33)]
    column = jnp.concatenate([taps_t[1056:1104, 128:256], jnp.zeros((16, 128), F32)], axis=0)
    step_c = iota((64, 128), 1) >> 4
    none = jnp.zeros((32, 128), F32)
    for shift in (1, 2, 4):
        stack = [
            jnp.where(
                (step & shift) > 0,
                stack[a - shift] if 0 <= a - shift else none,
                stack[a] if a < len(stack) else none,
            )
            for a in range(len(stack) + shift)
        ]
        column = jnp.where((step_c & shift) > 0, pltpu.roll(column, shift, 0), column)
    for a in range(56):
        inside = 8 <= a < 8 + len(stack)
        ws_ref[32 * a : 32 * a + 32, :] = stack[a - 8].astype(BF16) if inside else blank
    wcs_ref[...] = jnp.concatenate([column, pltpu.roll(column, 8, 0)], axis=1).astype(BF16)
    x = iota((128, 128), 0)
    y = iota((128, 128), 1)
    turn = jnp.where(((x >> 5) == (y >> 5)) & ((x & 31) + (y & 31) == 31), 1.0, 0.0).astype(BF16)
    turn_last = jnp.where(
        ((x < 32) & (x + y == 31)) | ((x >= 32) & (x == y)), 1.0, 0.0
    ).astype(BF16)
    turned = [
        jnp.dot(
            taps_f[0:144, 128 * c : 128 * c + 128].astype(BF16),
            turn_last if c == 8 else turn,
            preferred_element_type=F32,
        )
        for c in range(9)
    ]
    lane_w = iota((144, 128), 1)
    final = pltpu.roll(turned[8], 96, 1)
    final = jnp.where(lane_w < 33, final, 0.0)
    turned[8] = jnp.where(lane_w < 32, turned[8], 0.0)
    base = jnp.concatenate(turned, axis=1)
    for w in range(4):
        wf_ref[144 * w : 144 * w + 144, 0:1152] = (
            pltpu.roll(base, 32 * w, 1) if w else base
        ).astype(BF16)
        wf_ref[144 * w : 144 * w + 144, 1152:1280] = (
            pltpu.roll(final, w, 1) if w else final
        ).astype(BF16)

    thr = thrs_ref[...]
    eigs = jnp.concatenate([eig] * 4, axis=0)
    scales = 2.0 * eigs * norm_scale

    def imaged(source, start, ones, tgt, wgt):
        field = jnp.dot(
            wf_ref[:, 0:1024], source[start : start + 1024, :], preferred_element_type=F32
        )
        tail = jnp.concatenate([source[start + 1024 : start + 1152, :], ones], axis=0)
        field += jnp.dot(wf_ref[:, 1024:1200], tail, preferred_element_type=F32)
        power = eigs * (field * field)
        planes = jnp.sum(power.reshape(12, 48, 256), axis=1)
        printed = 1.0 / (1.0 + jnp.exp(-STEEP * (norm_scale * planes - thr)))
        tgt = jnp.concatenate([tgt[v // 3 : v // 3 + 1] for v in range(12)], axis=0)
        wgt = jnp.concatenate([wgt[v // 3 : v // 3 + 1] for v in range(12)], axis=0)
        slopes = wgt * 2.0 * (printed - tgt) * STEEP * printed * (1.0 - printed)
        adjoint = (scales.reshape(12, 48, 1) * slopes[:, None, :]) * field.reshape(12, 48, 256)
        return printed, adjoint.reshape(4, 144, 256).astype(BF16)

    for m in range(8):
        both = [
            jnp.concatenate(
                [tgt_main[kind, 4 * m : 4 * m + 4, :], tgt_main[kind, 4 * m + 32 : 4 * m + 36, :]],
                axis=1,
            )
            for kind in range(2)
        ]
        ones = e_ref[48 * m : 48 * m + 48, :]
        printed, adjoint = imaged(main_t, 128 * m, ones, *both)
        main_a[4 * m : 4 * m + 4] = adjoint[:, :, 0:128]
        main_a[4 * m + 32 : 4 * m + 36] = adjoint[:, :, 128:256]
        for v in range(12):
            w = 4 * m + v // 3
            res_main[v % 3, w : w + 1, :] = printed[v : v + 1, 0:128]
            res_main[v % 3, w + 32 : w + 33, :] = printed[v : v + 1, 128:256]

    for m in range(2):
        both = [tgt_side[kind, 4 * m : 4 * m + 4, :] for kind in range(2)]
        ones = e_ref[48 * (8 + m) : 48 * (9 + m), :]
        printed, adjoint = imaged(side_t, 128 * m, ones, *both)
        side_a[4 * m : 4 * m + 4] = adjoint
        for v in range(12):
            w = 4 * m + v // 3
            res_side[v % 3, w : w + 1, :] = printed[v : v + 1, :]

    for f in range(3):
        edge = jnp.concatenate(
            [res_side[f, :, 32 * g : 32 * g + 16] for g in range(2, 6)], axis=0
        )
        resist_ref[f] = jnp.concatenate([res_main[f, 16:48, 16:128], edge], axis=1)

    d_ref[...] = jnp.zeros_like(d_ref)
    d_last[...] = jnp.zeros_like(d_last)
    for i in (28, 32, *range(0, 28, 4), *range(36, 64, 4)):
        quad = jnp.concatenate(
            [
                jnp.concatenate([main_a[i, 0:128], main_a[i + 2, 0:128]], axis=1),
                jnp.concatenate([main_a[i + 1, 0:128], main_a[i + 3, 0:128]], axis=1),
            ],
            axis=0,
        )
        first, final = max(0, 30 - i), min(33, 63 - i)
        size = 32 * (final + 1 - first)
        left = jnp.concatenate(
            [
                jnp.concatenate(
                    [
                        wt_ref[32 * first + 32 : 32 * first + 32 + size, :],
                        wt_ref[32 * first : 32 * first + size, :],
                    ],
                    axis=1,
                ),
                wc_ref[...],
            ],
            axis=0,
        )
        part = jnp.dot(left, quad, preferred_element_type=F32)
        spot = 32 * (i + first - 30)
        if i == 28:
            h_main[0:1024, :] = part[0:size]
        elif i == 32:
            h_main[64:1024, :] += part[0:960]
            h_main[1024:1088, :] = part[960:1024]
        else:
            h_main[spot : spot + size, :] += part[0:size]
        d_ref[i : i + 48, :] += part[size:]
    for t in range(2):
        rest = jnp.concatenate(
            [
                jnp.concatenate(
                    [main_a[32 * t + r, 128:144], main_a[32 * t + 16 + r, 128:144]], axis=1
                )
                for r in range(16)
            ],
            axis=0,
        )
        first = 16 - 16 * t
        left = jnp.concatenate(
            [
                jnp.concatenate(
                    [
                        ws_ref[32 * first + 256 : 32 * first + 1280, :],
                        ws_ref[32 * first : 32 * first + 1024, :],
                    ],
                    axis=1,
                ),
                wcs_ref[...],
            ],
            axis=0,
        )
        part = jnp.dot(left, rest, preferred_element_type=F32)
        if t == 0:
            h_last[0:1024, :] = part[0:1024]
        else:
            h_last[512:1024, :] += part[0:512]
            h_last[1024:1536, :] = part[512:1024]
        d_last[32 * t : 32 * t + 64, :] += part[1024:]
    rest = jnp.concatenate([side_a[w, 128:144] for w in range(8)], axis=0)
    h_side[...] = jnp.dot(ws_ref[256:1536, :], rest, preferred_element_type=F32)
    for w in range(0, 8, 2):
        pair = jnp.concatenate([side_a[w, 0:128], side_a[w + 1, 0:128]], axis=0)
        left = jnp.concatenate([wt_ref[32:1120, :], wt_ref[0:1088, :]], axis=1)
        h_side[32 * w : 32 * w + 1088, :] += jnp.dot(left, pair, preferred_element_type=F32)

    group = lane >> 5
    for r in range(32):
        body = (
            h_main[32 * r + 64 : 32 * r + 96, 0:128]
            + h_main[32 * r : 32 * r + 32, 128:256]
            + h_last[32 * r + 512 : 32 * r + 544, 0:128]
            + h_last[32 * r : 32 * r + 32, 128:256]
        )
        edge = None
        for half in range(2):
            chosen = None
            for g in range(4 * half, 4 * half + 4):
                u = r + 32 - 8 * g
                if 0 <= u <= 39:
                    term = h_side[32 * u : 32 * u + 32, 128 * half : 128 * half + 128]
                    chosen = jnp.where(group == g % 4, term, 0.0 if chosen is None else chosen)
            edge = chosen if edge is None else edge + chosen
        edge = edge + pltpu.roll(edge, 64, 1)
        edge = edge + pltpu.roll(edge, 32, 1)
        both = jnp.where(lane < 32 - tap, edge, body)
        both = pltpu.roll(both, 96, 1, stride=1, stride_axis=0)
        grad_ref[r : r + 1, :] = (
            jnp.sum(both, axis=0, keepdims=True)
            + d_ref[r + 32 : r + 33, 0:128]
            + d_ref[r + 30 : r + 31, 128:256]
            + d_last[r + 32 : r + 33, 0:128]
            + d_last[r + 16 : r + 17, 128:256]
        )


VMEM_SPEC = pl.BlockSpec(memory_space=pltpu.VMEM)


def own_call(*given):
    return pl.pallas_call(
        own_kernel,
        out_shape=(
            jax.ShapeDtypeStruct((1024, 128), BF16),
            jax.ShapeDtypeStruct((256, 256), BF16),
            jax.ShapeDtypeStruct((144, 128), F32),
            jax.ShapeDtypeStruct((12, 256), F32),
        ),
        in_specs=[pl.BlockSpec(memory_space=pl.ANY)] * 3 + [VMEM_SPEC],
        out_specs=(VMEM_SPEC,) * 4,
        scratch_shapes=[
            pltpu.VMEM((8, 128), F32),
            pltpu.VMEM((32, 256), F32),
            pltpu.VMEM((1, 3), F32),
            pltpu.VMEM((1, 72), jnp.int32),
            pltpu.VMEM((1, 72), F32),
            pltpu.SemaphoreType.DMA((3,)),
        ],
        cost_estimate=pl.CostEstimate(flops=2**31, bytes_accessed=2**18, transcendentals=0),
        compiler_params=pltpu.CompilerParams(vmem_limit_bytes=16 * 1024 * 1024),
    )(*given)


def spread_call(*given):
    return pl.pallas_call(
        spread_kernel,
        out_shape=(
            jax.ShapeDtypeStruct((2048, 256), BF16),
            jax.ShapeDtypeStruct((1280, 256), BF16),
            jax.ShapeDtypeStruct((480, 256), BF16),
            jax.ShapeDtypeStruct((2, 64, 128), F32),
            jax.ShapeDtypeStruct((2, 8, 256), F32),
        ),
        in_specs=[VMEM_SPEC] * 6,
        out_specs=(VMEM_SPEC,) * 5,
        scratch_shapes=[
            pltpu.VMEM((112, 256), F32),
            pltpu.VMEM((56, 256), F32),
            pltpu.VMEM((56, 256), F32),
            pltpu.VMEM((32, 352), F32),
            pltpu.VMEM((32, 352), F32),
        ],
        cost_estimate=pl.CostEstimate(flops=2**29, bytes_accessed=2**21, transcendentals=0),
        compiler_params=pltpu.CompilerParams(vmem_limit_bytes=16 * 1024 * 1024),
    )(*given)


def step_call(spread, order, four, other):
    return pl.pallas_call(
        step_kernel,
        out_shape=(
            jax.ShapeDtypeStruct((32, 128), F32),
            jax.ShapeDtypeStruct((3, 32, 128), F32),
        ),
        in_specs=[VMEM_SPEC] * 10,
        out_specs=(VMEM_SPEC, VMEM_SPEC),
        scratch_shapes=[
            pltpu.VMEM((256, 1152), BF16),
            pltpu.VMEM((576, 1280), BF16),
            pltpu.VMEM((1120, 128), BF16),
            pltpu.VMEM((48, 256), BF16),
            pltpu.VMEM((1792, 128), BF16),
            pltpu.VMEM((64, 256), BF16),
            pltpu.VMEM((64, 144, 128), BF16),
            pltpu.VMEM((8, 144, 256), BF16),
            pltpu.VMEM((1088, 256), F32),
            pltpu.VMEM((1536, 256), F32),
            pltpu.VMEM((1280, 256), F32),
            pltpu.VMEM((112, 256), F32),
            pltpu.VMEM((96, 256), F32),
            pltpu.VMEM((3, 64, 128), F32),
            pltpu.VMEM((3, 8, 256), F32),
        ],
        compiler_params=pltpu.CompilerParams(vmem_limit_bytes=32 * 1024 * 1024),
    )(*spread, *order, four, other)


def flat_taps(kernels):
    count = kernels.shape[0] * 2
    pairs = kernels.reshape(count, 33, 33)
    return jnp.concatenate(
        [
            pairs[:, :, :32].reshape(count, 1056),
            pairs[:, :, 32],
            jnp.zeros((count, 63), BF16),
        ],
        axis=1,
    )


def on_device(mask, kernels, eigen, focus, target, pixel_weight, threshold):
    strips = lax.axis_size("strip")
    me = lax.axis_index("kern")

    odd = lax.axis_index("strip") % 2

    def columns(array, rim, row=0, count=32):
        wide = jnp.pad(array.astype(F32), ((0, 0), (rim, rim)))
        return lax.dynamic_slice(wide, (row, me * 128), (count, 128 + 2 * rim))

    def rim_rows(row):
        edges = [columns(target, 16, row, 16), columns(pixel_weight, 16, row, 16)]
        return jnp.concatenate([columns(mask, 32), jnp.concatenate(edges, axis=0)], axis=1)

    near_pairs = [(i, i ^ 1) for i in range(strips)]
    far_pairs = []
    for k in range(8):
        for i in range(strips):
            if i in (0, strips - 1):
                far_pairs.append((k * strips + i, (k ^ 1) * strips + i))
            else:
                far_pairs.append((k * strips + i, k * strips + ((i - 1) ^ 1) + 1))
    near = lax.ppermute(rim_rows(16 - 16 * odd), "strip", near_pairs)
    far = lax.ppermute(rim_rows(16 * odd), ("kern", "strip"), far_pairs)

    taps = flat_taps(kernels)
    four = jnp.concatenate(
        [taps]
        + [lax.ppermute(taps, "kern", [(i, i ^ (2 * s)) for i in range(8)]) for s in range(1, 4)]
    )
    beside = [
        (k * strips + s, (k ^ 1) * strips + (s ^ (strips // 2) if s % 2 else s))
        for k in range(8)
        for s in range(strips)
    ]
    other = lax.ppermute(four, ("kern", "strip"), beside)

    own_mask = columns(mask, 32)
    center, *order = own_call(
        threshold.reshape(1, 3), focus.reshape(1, 72), eigen.reshape(1, 72), own_mask
    )
    spread = spread_call(
        center, own_mask, columns(target, 16), columns(pixel_weight, 16), near, far
    )
    return step_call(spread, order, four, other)


def solution(mesh):
    placed = (
        P("strip", None),
        P("kern", None, None, None),
        P(),
        P(),
        P("strip", None),
        P("strip", None),
        P(),
    )
    return jax.shard_map(
        on_device,
        mesh=mesh,
        in_specs=placed,
        out_specs=(P("strip", "kern"), P(None, "strip", "kern")),
        check_vma=False,
    )
```

```python
import jax
import jax.numpy as jnp
from jax import lax
from jax.experimental import pallas as pl
from jax.experimental.pallas import tpu as pltpu
from jax.sharding import PartitionSpec as P

STEEP = 20.0
F32 = jnp.float32
BF16 = jnp.bfloat16


def iota(shape, dim):
    return lax.broadcasted_iota(jnp.int32, shape, dim)


def skewed(eight, j, tap, lane):
    left = jnp.broadcast_to(eight[j : j + 1, 0:128], (32, 128))
    right = jnp.broadcast_to(eight[j : j + 1, 128:256], (32, 128))
    left = pltpu.roll(left, 97, 1, stride=1, stride_axis=0)
    right = pltpu.roll(right, 97, 1, stride=1, stride_axis=0)
    return jnp.where(lane + 31 - tap < 128, left, right).astype(BF16)


def own_kernel(
    thr_ref, focus_ref, eigen_ref, mask_ref,
    center, pick_ref, eig_ref, thrs_ref,
    both_ref, rows_ref, thr_vm, focus_vm, eigen_vm, sems,
):
    me = lax.axis_index("kern")
    copies = [
        pltpu.make_async_copy(src, dst, sems.at[n])
        for n, (src, dst) in enumerate(
            ((thr_ref, thr_vm), (focus_ref, focus_vm), (eigen_ref, eigen_vm))
        )
    ]
    for copy in copies:
        copy.start()
    rows_ref[:, 128:256] = jnp.zeros((32, 128), F32)
    rows_ref[:, 0:192] = mask_ref[...]
    tap = iota((32, 128), 0)
    lane = iota((32, 128), 1)

    def spread_own(block, _):
        eight = rows_ref[pl.ds(pl.multiple_of(block * 8, 8), 8), :]
        for j in range(8):
            spot = pl.multiple_of((block * 8 + j) * 32, 32)
            center[pl.ds(spot, 32), :] = skewed(eight, j, tap, lane)
        return 0

    lax.fori_loop(0, 4, spread_own, 0)

    for copy in copies:
        copy.wait()
    both_ref[...] = jnp.zeros((8, 128), F32)
    both_ref[0:1, 0:72] = focus_vm[...].astype(F32)
    both_ref[1:2, 0:72] = eigen_vm[...]
    listed = jnp.transpose(both_ref[...])
    slot = iota((1, 256), 1)
    place = slot & 127
    block = (place >= 18).astype(jnp.int32) + (place >= 36) + (place >= 54)
    holder = me ^ (2 * block + (slot >> 7))
    inside = place < 72
    system = jnp.where(inside, 9 * holder + ((place - 18 * block) >> 1), -1)
    here = iota((128, 256), 0) == system
    frow = jnp.sum(jnp.where(here, listed[:, 0:1], 0.0), axis=0, keepdims=True)
    frow = jnp.where(inside, frow, -1.0)
    erow = jnp.sum(jnp.where(here, listed[:, 1:2], 0.0), axis=0, keepdims=True)
    fcol = jnp.transpose(jnp.broadcast_to(frow, (8, 256)))[:, 0:1]
    before = (fcol == frow) & (iota((256, 256), 0) < iota((256, 256), 1))
    rank = jnp.sum(jnp.where(before, 1.0, 0.0), axis=0, keepdims=True)
    pos = jnp.where(frow >= 0.0, frow * 48.0 + rank, -1.0)
    spot = iota((256, 256), 0)
    spot = jnp.where(spot < 128, spot, 128 + (spot & 15))
    pick = jnp.where(spot.astype(F32) == pos, 1.0, 0.0)
    pick_ref[...] = pick.astype(BF16)
    eig = jnp.sum(pick * erow, axis=1, keepdims=True)[0:144]
    eig_ref[...] = jnp.broadcast_to(eig, (144, 128))
    for v in range(12):
        thrs_ref[v : v + 1, :] = jnp.broadcast_to(thr_vm[0:1, v % 3 : v % 3 + 1], (1, 256))


def spread_kernel(
    center, mask_ref, target_ref, weight_ref, near_ref, far_ref,
    main_t, side_t, e_ref, tgt_main, tgt_side,
    rows_ref, lo_ref, hi_ref, up_ref, down_ref,
):
    strip = lax.axis_index("strip")
    last = lax.axis_size("strip") - 1

    odd = jnp.full((32, 352), strip & 1, jnp.int32) > 0
    up_ref[...] = jnp.where(odd, near_ref[...], far_ref[...])
    down_ref[...] = jnp.where(odd, far_ref[...], near_ref[...])

    has_up = (strip > 0).astype(F32)
    has_down = (strip < last).astype(F32)
    rows_ref[96:, :] = jnp.zeros((16, 256), F32)
    rows_ref[:, 128:] = jnp.zeros((112, 128), F32)
    rows_ref[0:32, 0:192] = up_ref[:, 0:192] * has_up
    rows_ref[32:64, 0:192] = mask_ref[...]
    rows_ref[64:96, 0:192] = down_ref[:, 0:192] * has_down

    for kind in range(2):
        above = up_ref[16 * kind : 16 * kind + 16, 192:352]
        below = down_ref[16 * kind : 16 * kind + 16, 192:352]
        if kind == 1:
            above = above * has_up
            below = below * has_down
        mine = (weight_ref if kind else target_ref)[...]
        area = jnp.concatenate([above, mine, below], axis=0)
        tgt_main[kind] = area[:, 0:128]
        tgt_side[kind] = jnp.concatenate(
            [area[8 * g : 8 * g + 8, 128:160] for g in range(8)], axis=1
        )

    lo_ref[...] = jnp.concatenate([rows_ref[8 * g : 8 * g + 56, 128:160] for g in range(8)], axis=1)
    hi_ref[...] = jnp.concatenate([rows_ref[8 * g : 8 * g + 56, 160:192] for g in range(8)], axis=1)

    tap = iota((32, 128), 0)
    lane = iota((32, 128), 1)

    main_t[1024:2048, 0:128] = center[...]
    main_t[0:1024, 128:256] = center[...]

    def spread_rim(block, _):
        start = pl.multiple_of(block * 8, 8)
        above, below = rows_ref[pl.ds(start, 8), :], rows_ref[pl.ds(start + 64, 8), :]
        for j in range(8):
            spot = pl.multiple_of((block * 8 + j) * 32, 32)
            main_t[pl.ds(spot, 32), 0:128] = skewed(above, j, tap, lane)
            main_t[pl.ds(spot + 1024, 32), 128:256] = skewed(below, j, tap, lane)
        return 0

    lax.fori_loop(0, 4, spread_rim, 0)

    def spread_side(block, _):
        start = pl.multiple_of(block * 8, 8)
        lows, highs = lo_ref[pl.ds(start, 8), :], hi_ref[pl.ds(start, 8), :]
        for j in range(8):
            for half in range(2):
                cols = slice(128 * half, 128 * half + 128)
                low = jnp.broadcast_to(lows[j : j + 1, cols], (32, 128))
                high = jnp.broadcast_to(highs[j : j + 1, cols], (32, 128))
                low = pltpu.roll(low, 97, 1, stride=1, stride_axis=0)
                high = pltpu.roll(high, 1, 1, stride=1, stride_axis=0)
                both = jnp.where((lane & 31) <= tap, low, high).astype(BF16)
                side_t[pl.ds(pl.multiple_of((block * 8 + j) * 32, 32), 32), cols] = both
        return 0

    lax.fori_loop(0, 5, spread_side, 0)

    for m in range(8):
        e_ref[48 * m : 48 * m + 48, :] = jnp.concatenate(
            [rows_ref[4 * m : 4 * m + 48, 32:160], rows_ref[4 * m + 32 : 4 * m + 80, 32:160]], axis=1
        ).astype(BF16)
    for m in range(2):
        e_ref[48 * (8 + m) : 48 * (9 + m), :] = hi_ref[4 * m : 4 * m + 48, :].astype(BF16)


def step_kernel(
    main_t, side_t, e_ref, tgt_main, tgt_side, pick_ref, eig_ref, thrs_ref, four_ref, other_ref,
    grad_ref, resist_ref,
    raw_ref, wf_ref, wt_ref, wc_ref, ws_ref, wcs_ref, main_a, side_a,
    h_main, h_last, h_side, d_ref, d_last, res_main, res_side,
):
    norm_scale = 3.0 / 72
    tap = iota((32, 128), 0)
    lane = iota((32, 128), 1)
    eig = eig_ref[:, 0:1]

    raw_ref[...] = jnp.zeros_like(raw_ref)
    raw_ref[0:72, :] = four_ref[...]
    raw_ref[128:200, :] = other_ref[...]
    taps_f = jnp.dot(pick_ref[...], raw_ref[...], preferred_element_type=F32)
    taps_t = jnp.transpose(taps_f)
    blank = jnp.zeros((32, 128), BF16)
    wt_ref[0:32, :] = blank
    wt_ref[32:1088, :] = taps_t[0:1056, 0:128].astype(BF16)
    wt_ref[1088:1120, :] = blank
    edge_taps = taps_t[1056:1104, 0:128]
    wc_ref[...] = jnp.concatenate([edge_taps, pltpu.roll(edge_taps, 1, 0)], axis=1).astype(BF16)
    step = lane >> 4
    stack = [taps_t[32 * a : 32 * a + 32, 128:256] for a in range(33)]
    column = jnp.concatenate([taps_t[1056:1104, 128:256], jnp.zeros((16, 128), F32)], axis=0)
    step_c = iota((64, 128), 1) >> 4
    none = jnp.zeros((32, 128), F32)
    for shift in (1, 2, 4):
        stack = [
            jnp.where(
                (step & shift) > 0,
                stack[a - shift] if 0 <= a - shift else none,
                stack[a] if a < len(stack) else none,
            )
            for a in range(len(stack) + shift)
        ]
        column = jnp.where((step_c & shift) > 0, pltpu.roll(column, shift, 0), column)
    for a in range(56):
        inside = 8 <= a < 8 + len(stack)
        ws_ref[32 * a : 32 * a + 32, :] = stack[a - 8].astype(BF16) if inside else blank
    wcs_ref[...] = jnp.concatenate([column, pltpu.roll(column, 8, 0)], axis=1).astype(BF16)
    x = iota((128, 128), 0)
    y = iota((128, 128), 1)
    turn = jnp.where(((x >> 5) == (y >> 5)) & ((x & 31) + (y & 31) == 31), 1.0, 0.0).astype(BF16)
    turn_last = jnp.where(
        ((x < 32) & (x + y == 31)) | ((x >= 32) & (x == y)), 1.0, 0.0
    ).astype(BF16)
    turned = [
        jnp.dot(
            taps_f[0:144, 128 * c : 128 * c + 128].astype(BF16),
            turn_last if c == 8 else turn,
            preferred_element_type=F32,
        )
        for c in range(9)
    ]
    lane_w = iota((144, 128), 1)
    final = pltpu.roll(turned[8], 96, 1)
    final = jnp.where(lane_w < 33, final, 0.0)
    turned[8] = jnp.where(lane_w < 32, turned[8], 0.0)
    base = jnp.concatenate(turned, axis=1)
    for w in range(4):
        wf_ref[144 * w : 144 * w + 144, 0:1152] = (
            pltpu.roll(base, 32 * w, 1) if w else base
        ).astype(BF16)
        wf_ref[144 * w : 144 * w + 144, 1152:1280] = (
            pltpu.roll(final, w, 1) if w else final
        ).astype(BF16)

    thr = thrs_ref[...]
    eigs = jnp.concatenate([eig] * 4, axis=0)
    scales = 2.0 * eigs * norm_scale

    def imaged(source, start, ones, tgt, wgt):
        window = jnp.concatenate([source[start : start + 1152, :], ones], axis=0)
        field = jnp.dot(wf_ref[:, 0:1200], window, preferred_element_type=F32)
        power = eigs * (field * field)
        planes = jnp.sum(power.reshape(12, 48, 256), axis=1)
        printed = 1.0 / (1.0 + jnp.exp(-STEEP * (norm_scale * planes - thr)))
        tgt = jnp.concatenate([tgt[v // 3 : v // 3 + 1] for v in range(12)], axis=0)
        wgt = jnp.concatenate([wgt[v // 3 : v // 3 + 1] for v in range(12)], axis=0)
        slopes = wgt * 2.0 * (printed - tgt) * STEEP * printed * (1.0 - printed)
        adjoint = (scales.reshape(12, 48, 1) * slopes[:, None, :]) * field.reshape(12, 48, 256)
        return printed, adjoint.reshape(4, 144, 256).astype(BF16)

    for m in range(8):
        both = [
            jnp.concatenate(
                [tgt_main[kind, 4 * m : 4 * m + 4, :], tgt_main[kind, 4 * m + 32 : 4 * m + 36, :]],
                axis=1,
            )
            for kind in range(2)
        ]
        ones = e_ref[48 * m : 48 * m + 48, :]
        printed, adjoint = imaged(main_t, 128 * m, ones, *both)
        main_a[4 * m : 4 * m + 4] = adjoint[:, :, 0:128]
        main_a[4 * m + 32 : 4 * m + 36] = adjoint[:, :, 128:256]
        for v in range(12):
            w = 4 * m + v // 3
            res_main[v % 3, w : w + 1, :] = printed[v : v + 1, 0:128]
            res_main[v % 3, w + 32 : w + 33, :] = printed[v : v + 1, 128:256]

    for m in range(2):
        both = [tgt_side[kind, 4 * m : 4 * m + 4, :] for kind in range(2)]
        ones = e_ref[48 * (8 + m) : 48 * (9 + m), :]
        printed, adjoint = imaged(side_t, 128 * m, ones, *both)
        side_a[4 * m : 4 * m + 4] = adjoint
        for v in range(12):
            w = 4 * m + v // 3
            res_side[v % 3, w : w + 1, :] = printed[v : v + 1, :]

    for f in range(3):
        edge = jnp.concatenate(
            [res_side[f, :, 32 * g : 32 * g + 16] for g in range(2, 6)], axis=0
        )
        resist_ref[f] = jnp.concatenate([res_main[f, 16:48, 16:128], edge], axis=1)

    d_ref[...] = jnp.zeros_like(d_ref)
    d_last[...] = jnp.zeros_like(d_last)
    for i in (28, 32, *range(0, 28, 4), *range(36, 64, 4)):
        quad = jnp.concatenate(
            [
                jnp.concatenate([main_a[i, 0:128], main_a[i + 2, 0:128]], axis=1),
                jnp.concatenate([main_a[i + 1, 0:128], main_a[i + 3, 0:128]], axis=1),
            ],
            axis=0,
        )
        first, final = max(0, 30 - i), min(33, 63 - i)
        size = 32 * (final + 1 - first)
        left = jnp.concatenate(
            [
                jnp.concatenate(
                    [
                        wt_ref[32 * first + 32 : 32 * first + 32 + size, :],
                        wt_ref[32 * first : 32 * first + size, :],
                    ],
                    axis=1,
                ),
                wc_ref[...],
            ],
            axis=0,
        )
        part = jnp.dot(left, quad, preferred_element_type=F32)
        spot = 32 * (i + first - 30)
        if i == 28:
            h_main[0:1024, :] = part[0:size]
        elif i == 32:
            h_main[64:1024, :] += part[0:960]
            h_main[1024:1088, :] = part[960:1024]
        else:
            h_main[spot : spot + size, :] += part[0:size]
        d_ref[i : i + 48, :] += part[size:]
    for t in range(2):
        rest = jnp.concatenate(
            [
                jnp.concatenate(
                    [main_a[32 * t + r, 128:144], main_a[32 * t + 16 + r, 128:144]], axis=1
                )
                for r in range(16)
            ],
            axis=0,
        )
        first = 16 - 16 * t
        left = jnp.concatenate(
            [
                jnp.concatenate(
                    [
                        ws_ref[32 * first + 256 : 32 * first + 1280, :],
                        ws_ref[32 * first : 32 * first + 1024, :],
                    ],
                    axis=1,
                ),
                wcs_ref[...],
            ],
            axis=0,
        )
        part = jnp.dot(left, rest, preferred_element_type=F32)
        if t == 0:
            h_last[0:1024, :] = part[0:1024]
        else:
            h_last[512:1024, :] += part[0:512]
            h_last[1024:1536, :] = part[512:1024]
        d_last[32 * t : 32 * t + 64, :] += part[1024:]
    rest = jnp.concatenate([side_a[w, 128:144] for w in range(8)], axis=0)
    h_side[...] = jnp.dot(ws_ref[256:1536, :], rest, preferred_element_type=F32)
    for w in range(0, 8, 2):
        pair = jnp.concatenate([side_a[w, 0:128], side_a[w + 1, 0:128]], axis=0)
        left = jnp.concatenate([wt_ref[32:1120, :], wt_ref[0:1088, :]], axis=1)
        h_side[32 * w : 32 * w + 1088, :] += jnp.dot(left, pair, preferred_element_type=F32)

    group = lane >> 5
    for r in range(32):
        body = (
            h_main[32 * r + 64 : 32 * r + 96, 0:128]
            + h_main[32 * r : 32 * r + 32, 128:256]
            + h_last[32 * r + 512 : 32 * r + 544, 0:128]
            + h_last[32 * r : 32 * r + 32, 128:256]
        )
        edge = None
        for half in range(2):
            chosen = None
            for g in range(4 * half, 4 * half + 4):
                u = r + 32 - 8 * g
                if 0 <= u <= 39:
                    term = h_side[32 * u : 32 * u + 32, 128 * half : 128 * half + 128]
                    chosen = jnp.where(group == g % 4, term, 0.0 if chosen is None else chosen)
            edge = chosen if edge is None else edge + chosen
        edge = edge + pltpu.roll(edge, 64, 1)
        edge = edge + pltpu.roll(edge, 32, 1)
        body = pltpu.roll(body, 96, 1, stride=1, stride_axis=0)
        edge = pltpu.roll(edge, 96, 1, stride=1, stride_axis=0)
        both = jnp.where(lane + 32 - tap < 128, body, edge)
        grad_ref[r : r + 1, :] = (
            jnp.sum(both, axis=0, keepdims=True)
            + d_ref[r + 32 : r + 33, 0:128]
            + d_ref[r + 30 : r + 31, 128:256]
            + d_last[r + 32 : r + 33, 0:128]
            + d_last[r + 16 : r + 17, 128:256]
        )


VMEM_SPEC = pl.BlockSpec(memory_space=pltpu.VMEM)


def own_call(*given):
    return pl.pallas_call(
        own_kernel,
        out_shape=(
            jax.ShapeDtypeStruct((1024, 128), BF16),
            jax.ShapeDtypeStruct((256, 256), BF16),
            jax.ShapeDtypeStruct((144, 128), F32),
            jax.ShapeDtypeStruct((12, 256), F32),
        ),
        in_specs=[pl.BlockSpec(memory_space=pl.ANY)] * 3 + [VMEM_SPEC],
        out_specs=(VMEM_SPEC,) * 4,
        scratch_shapes=[
            pltpu.VMEM((8, 128), F32),
            pltpu.VMEM((32, 256), F32),
            pltpu.VMEM((1, 3), F32),
            pltpu.VMEM((1, 72), jnp.int32),
            pltpu.VMEM((1, 72), F32),
            pltpu.SemaphoreType.DMA((3,)),
        ],
        cost_estimate=pl.CostEstimate(flops=2**31, bytes_accessed=2**18, transcendentals=0),
        compiler_params=pltpu.CompilerParams(vmem_limit_bytes=16 * 1024 * 1024),
    )(*given)


def spread_call(*given):
    return pl.pallas_call(
        spread_kernel,
        out_shape=(
            jax.ShapeDtypeStruct((2048, 256), BF16),
            jax.ShapeDtypeStruct((1280, 256), BF16),
            jax.ShapeDtypeStruct((480, 256), BF16),
            jax.ShapeDtypeStruct((2, 64, 128), F32),
            jax.ShapeDtypeStruct((2, 8, 256), F32),
        ),
        in_specs=[VMEM_SPEC] * 6,
        out_specs=(VMEM_SPEC,) * 5,
        scratch_shapes=[
            pltpu.VMEM((112, 256), F32),
            pltpu.VMEM((56, 256), F32),
            pltpu.VMEM((56, 256), F32),
            pltpu.VMEM((32, 352), F32),
            pltpu.VMEM((32, 352), F32),
        ],
        cost_estimate=pl.CostEstimate(flops=2**29, bytes_accessed=2**21, transcendentals=0),
        compiler_params=pltpu.CompilerParams(vmem_limit_bytes=16 * 1024 * 1024),
    )(*given)


def step_call(spread, order, four, other):
    return pl.pallas_call(
        step_kernel,
        out_shape=(
            jax.ShapeDtypeStruct((32, 128), F32),
            jax.ShapeDtypeStruct((3, 32, 128), F32),
        ),
        in_specs=[VMEM_SPEC] * 10,
        out_specs=(VMEM_SPEC, VMEM_SPEC),
        scratch_shapes=[
            pltpu.VMEM((256, 1152), BF16),
            pltpu.VMEM((576, 1280), BF16),
            pltpu.VMEM((1120, 128), BF16),
            pltpu.VMEM((48, 256), BF16),
            pltpu.VMEM((1792, 128), BF16),
            pltpu.VMEM((64, 256), BF16),
            pltpu.VMEM((64, 144, 128), BF16),
            pltpu.VMEM((8, 144, 256), BF16),
            pltpu.VMEM((1088, 256), F32),
            pltpu.VMEM((1536, 256), F32),
            pltpu.VMEM((1280, 256), F32),
            pltpu.VMEM((112, 256), F32),
            pltpu.VMEM((96, 256), F32),
            pltpu.VMEM((3, 64, 128), F32),
            pltpu.VMEM((3, 8, 256), F32),
        ],
        compiler_params=pltpu.CompilerParams(vmem_limit_bytes=32 * 1024 * 1024),
    )(*spread, *order, four, other)


def flat_taps(kernels):
    count = kernels.shape[0] * 2
    pairs = kernels.reshape(count, 33, 33)
    return jnp.concatenate(
        [
            pairs[:, :, :32].reshape(count, 1056),
            pairs[:, :, 32],
            jnp.zeros((count, 63), BF16),
        ],
        axis=1,
    )


def on_device(mask, kernels, eigen, focus, target, pixel_weight, threshold):
    strips = lax.axis_size("strip")
    me = lax.axis_index("kern")

    odd = lax.axis_index("strip") % 2

    def columns(array, rim, row=0, count=32):
        wide = jnp.pad(array.astype(F32), ((0, 0), (rim, rim)))
        return lax.dynamic_slice(wide, (row, me * 128), (count, 128 + 2 * rim))

    def rim_rows(row):
        edges = [columns(target, 16, row, 16), columns(pixel_weight, 16, row, 16)]
        return jnp.concatenate([columns(mask, 32), jnp.concatenate(edges, axis=0)], axis=1)

    near_pairs = [(i, i ^ 1) for i in range(strips)]
    far_pairs = []
    for k in range(8):
        for i in range(strips):
            if i in (0, strips - 1):
                far_pairs.append((k * strips + i, (k ^ 1) * strips + i))
            else:
                far_pairs.append((k * strips + i, k * strips + ((i - 1) ^ 1) + 1))
    near = lax.ppermute(rim_rows(16 - 16 * odd), "strip", near_pairs)
    far = lax.ppermute(rim_rows(16 * odd), ("kern", "strip"), far_pairs)

    taps = flat_taps(kernels)
    four = jnp.concatenate(
        [taps]
        + [lax.ppermute(taps, "kern", [(i, i ^ (2 * s)) for i in range(8)]) for s in range(1, 4)]
    )
    beside = [
        (k * strips + s, (k ^ 1) * strips + (s ^ (strips // 2) if s % 2 else s))
        for k in range(8)
        for s in range(strips)
    ]
    other = lax.ppermute(four, ("kern", "strip"), beside)

    own_mask = columns(mask, 32)
    center, *order = own_call(
        threshold.reshape(1, 3), focus.reshape(1, 72), eigen.reshape(1, 72), own_mask
    )
    spread = spread_call(
        center, own_mask, columns(target, 16), columns(pixel_weight, 16), near, far
    )
    return step_call(spread, order, four, other)


def solution(mesh):
    placed = (
        P("strip", None),
        P("kern", None, None, None),
        P(),
        P(),
        P("strip", None),
        P("strip", None),
        P(),
    )
    return jax.shard_map(
        on_device,
        mesh=mesh,
        in_specs=placed,
        out_specs=(P("strip", "kern"), P(None, "strip", "kern")),
        check_vma=False,
    )
```
